32 devices in a mesh: groups: 2 (over y), expert: 16 (over z, x, core), tensor: 1.
Axes of the slice: x: 2, y: 2, z: 4, core: 2. Of those that a mesh axis runs over, the one named last changes fastest.
Arguments:
- tokens_one: bfloat16 [1024, 2048], P(('groups', 'expert', 'tensor')), parts along dimension 0, may hold values from -6 to 6
- tokens_two: bfloat16 [1024, 2048], P(('groups', 'expert', 'tensor')), parts along dimension 0, may hold values from -6 to 6
- experts_one: int32 [1024, 8], P(('groups', 'expert')), parts along dimension 0, may hold values from 0 to 15, all different within a row; in each aligned block of 32 rows (0 to 31, 32 to 63, ...) at most 24 rows name the same one
- experts_two: int32 [1024, 8], P(('groups', 'expert')), parts along dimension 0, may hold values from 0 to 15, all different within a row; in each aligned block of 32 rows (0 to 31, 32 to 63, ...) at most 24 rows name the same one
- gates_one: float32 [1024, 8], P(('groups', 'expert')), parts along dimension 0, may hold values from 0.02 to 1
- gates_two: float32 [1024, 8], P(('groups', 'expert')), parts along dimension 0, may hold values from 0.02 to 1
- old_placement: int32 [16], replicated, may hold values from 0 to 15, each once
- swap_flags: int32 [8], replicated, may hold values 0 or 1
- gate_up: bfloat16 [16, 2048, 2, 768], P('expert', None, None, 'tensor'), may hold values from -0.125 to 0.125
- down: bfloat16 [16, 768, 2048], P('expert', 'tensor'), may hold values from -0.21875 to 0.21875
Outputs:
- out_one: bfloat16 [1024, 2048], P(('groups', 'expert', 'tensor')), parts along dimension 0
- out_two: bfloat16 [1024, 2048], P(('groups', 'expert', 'tensor')), parts along dimension 0
- new_gate_up: bfloat16 [32, 2048, 2, 768], P(('groups', 'expert'), None, None, 'tensor'), parts along dimension 0
- new_down: bfloat16 [32, 768, 2048], P(('groups', 'expert'), 'tensor'), parts along dimension 0
The draws below stay inside these ranges and needn't reach their ends.
There are 2 independent parts, one for each index of `groups`. The reference program is written for one: setup_inputs(seed, part) draws one part's arguments, and reference() takes and returns one part's arrays. A program takes and returns all parts, laid end to end along the dimension named above; an argument that names none is the same for every part. Nothing has to cross between parts.
Inputs may be any that keep to these rules, and one draw needn't show every extreme that they name: `experts_one`: the ids of one row differ. In each aligned block of 32 rows no expert is named by more than 24 rows, a bound that some block reaches. `experts_two`: the ids of one row differ. In each aligned block of 32 rows no expert is named by more than 24 rows, a bound that some block reaches. `old_placement`: each expert appears once. `swap_flags`: entry p refers to the slots p and p + 8.
All inputs are finite; a program needn't handle non-finite values.
Results may differ from the reference program's by a relative error of at most 0.0058.
Values may be sent and summed in bfloat16 or wider, within the bound.
No kernel may reach another device: no remote copies, remote signals or barrier semaphores. Data moves between devices by JAX's collectives and lax.ppermute only.
A program may use at most 128 MiB of HBM per device.

```python
import math
import jax
import jax.numpy as jnp
import numpy as np
from jax import lax

D = 2048
FF = 768
TOP = 8
TOK_DEV = 32
EXPERTS = 16
TOKENS = 512
CAP = 24
N_EXPERT = 16
N_TENSOR = 1


def place_ends(drawn, rng, low, largest):
    index_at = [jax.random.randint(jax.random.fold_in(rng, axis), (), 0, length) for axis, length in enumerate(drawn.shape)]
    main_axis = drawn.shape.index(max(drawn.shape))
    next_to = index_at[:main_axis] + [(index_at[main_axis] + 1) % drawn.shape[main_axis]] + index_at[main_axis + 1:]
    return drawn.at[tuple(index_at)].set(low).at[tuple(next_to)].set(largest)


def block_scale(stream_key, shape, cuts, low, largest):
    factor_of, own = 1.0, jax.random.fold_in(stream_key, 6)
    for position, blocks in cuts:
        heights = jnp.exp(jax.random.uniform(jax.random.fold_in(own, position), (blocks,), jnp.float32, low / len(cuts), largest / len(cuts)))
        factor_of = factor_of * jnp.repeat(heights, shape[position] // blocks).reshape([-1 if axis == position else 1 for axis in range(len(shape))])
    return factor_of


def deal_out(key, own, number, rows, amount, top, bound, skew):
    ranking = jax.random.permutation(key, amount)
    crowded, common = portions_of(amount, rows * top, bound, skew, True), portions_of(amount, rows * top, bound, skew, False)
    places = jnp.arange(amount)

    def named(sizes, turn):
        used = int((sizes > 0).sum())
        fixed = max(1, used // 4)
        moved = fixed + (places - fixed + turn * (used - fixed)) % max(1, amount - fixed)
        return jnp.zeros((amount,), jnp.int32).at[ranking[jnp.where(places < fixed, places, moved)]].set(jnp.asarray(sizes, jnp.int32))

    sizes = jnp.where(number % 4 == 0, named(crowded, number // 4), named(common, number - number // 4 - 1))
    mixed = jax.random.permutation(jax.random.fold_in(own, 3), amount)
    giver, taker = mixed[0:amount // 2 * 2:2], mixed[1:amount // 2 * 2:2]
    room = jnp.minimum(sizes[giver] - 1, bound - sizes[taker]) // 2
    room = jnp.where((giver == ranking[0]) | (taker == ranking[0]) | (sizes[taker] == 0), 0, jnp.maximum(room, 0))
    moved = jax.random.randint(jax.random.fold_in(own, 4), (amount // 2,), 0, 1 << 20) % (room + 1)
    sizes = sizes.at[giver].add(-moved).at[taker].add(moved)
    labels = jnp.searchsorted(jnp.cumsum(sizes), jnp.arange(rows * top), side="right").astype(jnp.int32)
    table = labels.reshape(top, rows).T
    table = table[jax.random.permutation(jax.random.fold_in(own, 1), rows)]
    turn = jax.random.randint(jax.random.fold_in(own, 2), (rows, 1), 0, top)
    return jnp.take_along_axis(table, (jnp.arange(top)[None, :] + turn) % top, axis=1)


def portions_of(count, total, bound, lean, full):
    loads = [(1 << 20) // math.isqrt(standing ** lean) + 1 for standing in range(1, count + 1)]
    largest = bound if full else min(bound, max(-(-total // count), total * loads[0] // sum(loads)))
    least = 1 if total - largest >= count - 1 else 0
    given, rest = [largest] + [least] * (count - 1), total - largest - least * (count - 1)
    while rest > 0:
        movable = [i for i in range(1, count) if given[i] < largest] or [i for i in range(1, count) if given[i] < bound]
        mass, left = sum([loads[i] for i in movable]), rest
        for i in movable:
            extra = min(bound - given[i], max(1, left * loads[i] // mass), rest)
            given[i] = given[i] + extra
            rest = rest - extra
    return np.array(given)


def centred(stream_key, dims, deviation, most, pieces=(), kind=jnp.bfloat16):
    values = jax.random.normal(stream_key, dims, jnp.float32) * deviation
    if len(pieces) > 0:
        values = block_scale(stream_key, dims, pieces, -0.22, 0.18) * values
    return jnp.clip(values, min=-most, max=most).astype(kind)


def setup_inputs(seed: int = 0, part: int = 0) -> dict:
    streams_of = jax.random.split(jax.random.key(seed), 11)
    part_splits = jax.random.split(jax.random.fold_in(streams_of[10], part), 11)
    tokens_one = centred(part_splits[0], (TOKENS, D), 1.0, 6.0, ((0, 16),))
    tokens_two = centred(part_splits[1], (TOKENS, D), 1.0, 6.0, ((0, 16),))
    experts_one_keys = jax.random.split(jax.random.fold_in(part_splits[2], 1), TOKENS // (N_TENSOR * TOK_DEV))
    experts_one_turns = jax.random.permutation(jax.random.fold_in(part_splits[2], 3), TOKENS // (N_TENSOR * TOK_DEV))
    experts_one = jax.vmap(lambda own, number: deal_out(jax.random.fold_in(part_splits[2], 2), own, number, N_TENSOR * TOK_DEV, EXPERTS, TOP, CAP, 2))(experts_one_keys, experts_one_turns).reshape((TOKENS, TOP))
    experts_two_keys = jax.random.split(jax.random.fold_in(part_splits[3], 1), TOKENS // (N_TENSOR * TOK_DEV))
    experts_two_turns = jax.random.permutation(jax.random.fold_in(part_splits[3], 3), TOKENS // (N_TENSOR * TOK_DEV))
    experts_two = jax.vmap(lambda own, number: deal_out(jax.random.fold_in(part_splits[3], 2), own, number, N_TENSOR * TOK_DEV, EXPERTS, TOP, CAP, 2))(experts_two_keys, experts_two_turns).reshape((TOKENS, TOP))
    gates_one = jnp.clip(jnp.exp(math.log(1.0) - 3.912023 * jax.random.uniform(part_splits[4], (TOKENS, TOP), jnp.float32) ** block_scale(part_splits[4], (TOKENS, TOP), ((0, 16),), -0.2, 0.2)), 0.02, 1.0)
    gates_two = jnp.clip(jnp.exp(math.log(1.0) - 3.912023 * jax.random.uniform(part_splits[5], (TOKENS, TOP), jnp.float32) ** block_scale(part_splits[5], (TOKENS, TOP), ((0, 16),), -0.2, 0.2)), 0.02, 1.0)
    old_placement = jax.random.permutation(streams_of[6], EXPERTS).astype(jnp.int32)
    swap_flags = place_ends((jax.random.randint(streams_of[7], (EXPERTS // 2,), 0, 2) < 1).astype(jnp.int32), jax.random.fold_in(streams_of[7], 1), 0, 1)
    gate_up = centred(streams_of[8], (EXPERTS, D, 2, FF), D ** -0.5, 0.125, ((0, 16),))
    down = centred(streams_of[9], (EXPERTS, FF, D), FF ** -0.5, 0.21875, ((0, 16),))
    return {"tokens_one": tokens_one, "tokens_two": tokens_two, "experts_one": experts_one, "experts_two": experts_two, "gates_one": gates_one, "gates_two": gates_two, "old_placement": old_placement, "swap_flags": swap_flags, "gate_up": gate_up, "down": down}


def expert_layer(tokens, chosen, weights, placement, gate_up, down):
    flat_ids = chosen.reshape(-1).astype(jnp.int32)
    flat_weights = weights.reshape(-1)
    slot_index = jnp.arange(EXPERTS, dtype=jnp.int32)
    slot_of = jnp.zeros((EXPERTS,), jnp.int32).at[placement.astype(jnp.int32)].set(slot_index)
    capacity_all = N_EXPERT * CAP
    block_rows = math.gcd(capacity_all, 256)
    half_width = FF // N_TENSOR

    def per_expert(expert, result):
        chosen_here = flat_ids == expert
        positions = jnp.nonzero(chosen_here, size=capacity_all, fill_value=0)[0].astype(jnp.int32)
        row_count = jnp.sum(chosen_here.astype(jnp.int32))
        slot = slot_of[expert]
        gate_up_w = gate_up[slot]
        down_w = down[slot]

        def per_block(block, accum):
            picked_ids = lax.dynamic_slice_in_dim(positions, (block * block_rows).astype(jnp.int32), block_rows)
            valid = (block * block_rows + jnp.arange(block_rows, dtype=jnp.int32)) < row_count
            token_ids = picked_ids // TOP
            token_rows = tokens[token_ids]
            summed = jnp.zeros((block_rows, D), jnp.float32)
            for piece in range(N_TENSOR):
                lower = piece * half_width
                gate_part = jnp.dot(token_rows, gate_up_w[:, 0, lower:lower + half_width], preferred_element_type=jnp.float32)
                up_part = jnp.dot(token_rows, gate_up_w[:, 1, lower:lower + half_width], preferred_element_type=jnp.float32)
                hidden = (jax.nn.silu(gate_part) * up_part).astype(jnp.bfloat16)
                output_rows = jnp.dot(hidden, down_w[lower:lower + half_width, :], preferred_element_type=jnp.float32)
                summed = summed + lax.optimization_barrier(output_rows.astype(jnp.bfloat16)).astype(jnp.float32)
            factor = jnp.where(valid, flat_weights[picked_ids], jnp.zeros((block_rows,), flat_weights.dtype))
            return accum.at[token_ids].add(factor[:, None] * summed)

        return lax.fori_loop(0, (row_count + block_rows - 1) // block_rows, per_block, result)

    result = lax.fori_loop(0, EXPERTS, per_expert, jnp.zeros((TOKENS, D), jnp.float32))
    return result.astype(jnp.bfloat16)


def reference(tokens_one, tokens_two, experts_one, experts_two, gates_one, gates_two, old_placement, swap_flags, gate_up, down):
    weights_one = gates_one / jnp.sum(gates_one, axis=-1, keepdims=True)
    weights_two = gates_two / jnp.sum(gates_two, axis=-1, keepdims=True)
    half_count = EXPERTS // 2
    slot_index = jnp.arange(EXPERTS, dtype=jnp.int32)
    partner = (slot_index + half_count) % EXPERTS
    swap_here = swap_flags[slot_index % half_count] == 1
    new_placement = jnp.where(swap_here, old_placement[partner], old_placement)
    new_gate_up = jnp.where(swap_here[:, None, None, None], gate_up[partner], gate_up)
    new_down = jnp.where(swap_here[:, None, None], down[partner], down)
    out_one = expert_layer(tokens_one, experts_one, weights_one, old_placement, gate_up, down)
    out_two = expert_layer(tokens_two, experts_two, weights_two, new_placement, new_gate_up, new_down)
    return (out_one, out_two, new_gate_up, new_down)
```

```python
import jax
import jax.numpy as jnp
from jax import lax
from jax.sharding import PartitionSpec as P

LANES = 128


def xor_pairs(count, mask):
    return [(source, source ^ mask) for source in range(count)]


def shift_pairs(count, shift):
    return [(source, (source + shift) % count) for source in range(count)]


def exchange(value, mask):
    return lax.ppermute(value, "expert", xor_pairs(lax.axis_size("expert"), mask))


def slot_table(placement, slot_index):
    match_table = placement[:, None] == slot_index[None, :]
    return jnp.sum(jnp.where(match_table, slot_index[:, None], 0), axis=0)


def expert_ffn(rows, joined_w, down_w):
    half_width = down_w.shape[0]
    projected = jnp.dot(rows, joined_w, preferred_element_type=jnp.float32)
    hidden = (jax.nn.silu(projected[:, :half_width]) * projected[:, half_width:]).astype(
        jnp.bfloat16
    )
    return jnp.dot(hidden, down_w, preferred_element_type=jnp.float32)


def routed_layer(pair_rows, chosen, gates, slot_of, joined_w, down_w):
    row_total = pair_rows.shape[0]
    width = pair_rows.shape[1]
    top_count = chosen.shape[1]
    peer_total = lax.axis_size("expert")
    capacity = min(row_total, max(2, 3 * row_total * top_count // (2 * peer_total)))
    norm_gates = gates / jnp.sum(gates, axis=-1, keepdims=True)
    slot_index = jnp.arange(peer_total, dtype=jnp.int32)
    flat_ids = chosen.reshape(-1)
    expert_hot = flat_ids[:, None] == slot_index[None, :]
    target = jnp.sum(jnp.where(expert_hot, slot_of[None, :], 0), axis=1)
    target_hot = target[:, None] == slot_index[None, :]
    running = jnp.cumsum(target_hot.astype(jnp.int32), axis=0)
    position = jnp.sum(jnp.where(target_hot, running, 0), axis=1) - 1
    outgoing = jnp.zeros((peer_total, capacity, width), jnp.bfloat16)
    outgoing = outgoing.at[target, position].set(jnp.repeat(pair_rows, top_count, axis=0))
    received = lax.all_to_all(outgoing, "expert", split_axis=0, concat_axis=0, tiled=True)
    partial_rows = expert_ffn(received.reshape(-1, width), joined_w, down_w).astype(jnp.bfloat16)
    returned = lax.all_to_all(
        partial_rows.reshape(received.shape), "expert", split_axis=0, concat_axis=0, tiled=True
    )
    picked = returned[target, position].astype(jnp.float32)
    weighted = picked * norm_gates.reshape(-1)[:, None]
    partial_value = jnp.sum(weighted.reshape(row_total, top_count, width), axis=1)
    return lax.psum_scatter(partial_value, "tensor", scatter_dimension=0, tiled=True).astype(
        jnp.bfloat16
    )


def extended_rows(rows, chosen, gates, placement):
    norm_gates = gates / jnp.sum(gates, axis=-1, keepdims=True)
    hot = chosen[:, :, None] == placement[None, None, :]
    dense = jnp.sum(jnp.where(hot, norm_gates[:, :, None], 0.0), axis=1)
    high = lax.reduce_precision(dense, 8, 7)
    middle = lax.reduce_precision(dense - high, 8, 7)
    low = dense - high - middle
    slots = placement.shape[0]
    spare = jnp.zeros((rows.shape[0], LANES - 3 * slots), jnp.bfloat16)
    parts = [part.astype(jnp.bfloat16) for part in (high, middle, low)]
    return jnp.concatenate([rows, *parts, spare], axis=1)


def weighted_ffn(piece, width, slots, joined_w, down_w):
    own_index = lax.axis_index("expert")
    tail = piece[:, width:].astype(jnp.float32)
    column = lax.broadcasted_iota(jnp.int32, tail.shape, 1)
    mine = (column % slots == own_index) & (column < 3 * slots)
    weight = jnp.sum(jnp.where(mine, tail, 0.0), axis=1, keepdims=True)
    return weight * expert_ffn(piece[:, :width], joined_w, down_w)


def half_piece(array, axis, half, index, count):
    rows = array.shape[axis] // (2 * count)
    return lax.dynamic_slice_in_dim(array, (half * count + index) * rows, rows, axis=axis)


def assemble(shape, axis, group, own_parts, other_parts):
    result = jnp.zeros(shape, jnp.bfloat16)
    count = len(own_parts)
    rows = shape[axis] // (2 * count)
    for parts, half in ((own_parts, group), (other_parts, 1 - group)):
        for index, part in enumerate(parts):
            start = (half * count + index) * rows
            result = lax.dynamic_update_slice_in_dim(result, part, start, axis=axis)
    return result


def swap_steps(on, group, gate_up, down, plan):
    half_bit = lax.axis_size("expert") // 2
    counts = (
        sum(1 for step in plan for name, _ in step if name == "g"),
        sum(1 for step in plan for name, _ in step if name == "d"),
    )
    arrived, relayed, pending = {}, {}, []

    def cut(item):
        name, index = item
        if name == "g":
            return half_piece(gate_up, 1, group, index, counts[0])
        return half_piece(down, 1, group, index, counts[1])

    def step(items, work):
        nonlocal pending
        outgoing = [cut(item) for item in items]
        to_relay = [arrived[item] for item in pending]

        def active(args):
            outgoing, to_relay = args
            crossed = [exchange(value, half_bit) for value in outgoing]
            handed = [lax.ppermute(value, "groups", [(0, 1), (1, 0)]) for value in to_relay]
            return crossed, handed, work()

        def idle(args):
            outgoing, to_relay = args
            return list(outgoing), list(to_relay), work()

        crossed, handed, made = lax.cond(on, active, idle, (outgoing, to_relay))
        for item, value in zip(pending, handed):
            relayed[item] = value
        for item, value in zip(items, crossed):
            arrived[item] = value
        pending = list(items)
        return made

    def finish():
        to_relay = [arrived[item] for item in pending]

        def active(to_relay):
            handed = [lax.ppermute(value, "groups", [(0, 1), (1, 0)]) for value in to_relay]
            for item, value in zip(pending, handed):
                relayed[item] = value
            whole = []
            for name, count, like in (("g", counts[0], gate_up), ("d", counts[1], down)):
                whole.append(
                    assemble(
                        like.shape,
                        1,
                        group,
                        [arrived[name, index] for index in range(count)],
                        [relayed[name, index] for index in range(count)],
                    )
                )
            return tuple(whole)

        return lax.cond(on, active, lambda _: (gate_up, down), to_relay)

    return step, finish


PLAN = (
    (("g", 0),),
    (("g", 1), ("d", 0)),
    (("g", 2),),
    (("g", 3), ("d", 1)),
)


def staged(
    tokens, chosen, gates, placement, gate_up, down, step, finish
):
    peers = lax.axis_size("expert")
    levels = peers // 4
    rows, width = tokens.shape
    own = extended_rows(tokens, chosen, gates, placement)

    joined = lambda: gate_up[0].reshape(width, -1)
    ffn = lambda piece, joined_w: weighted_ffn(piece, width, peers, joined_w, down[0])

    columns = [own] + [
        lax.ppermute(own, "expert", shift_pairs(peers, 4 * hop)) for hop in range(1, levels)
    ]
    joined_w = step(PLAN[0], joined)
    here = jnp.concatenate(columns, axis=0)
    across = exchange(here, 2)
    here_core = exchange(here, 1)
    part_here, part_here_core = step(
        PLAN[1], lambda: (ffn(here, joined_w), ffn(here_core, joined_w).astype(jnp.bfloat16))
    )
    across_core = exchange(across, 1)
    got_here = exchange(part_here_core, 1)
    part_across, part_across_core = step(
        PLAN[2],
        lambda: (ffn(across, joined_w), ffn(across_core, joined_w).astype(jnp.bfloat16)),
    )
    got_across = exchange(part_across_core, 1)
    sum_across = (part_across + got_across.astype(jnp.float32)).astype(jnp.bfloat16)
    got_column = exchange(sum_across, 2)
    sum_here = step(PLAN[3], lambda: part_here + got_here.astype(jnp.float32))
    column = sum_here + got_column.astype(jnp.float32)
    total = column[:rows]
    returned = [
        lax.ppermute(
            column[hop * rows : (hop + 1) * rows].astype(jnp.bfloat16),
            "expert",
            shift_pairs(peers, peers - 4 * hop),
        )
        for hop in range(1, levels)
    ]
    new_gate_up, new_down = finish()
    for value in returned:
        total = total + value.astype(jnp.float32)
    total = total.astype(jnp.bfloat16)
    return total, new_gate_up, new_down


def body(
    tokens_one,
    tokens_two,
    experts_one,
    experts_two,
    gates_one,
    gates_two,
    old_placement,
    swap_flags,
    gate_up,
    down,
):
    peer_total = lax.axis_size("expert")
    half_count = peer_total // 2
    own_index = lax.axis_index("expert")
    group = lax.axis_index("groups")
    swap_here = swap_flags[own_index % half_count] == 1
    step, finish = swap_steps(swap_here, group, gate_up, down, PLAN)
    if lax.axis_size("tensor") == 1 and peer_total == 16:
        count = tokens_one.shape[0]
        total, new_gate_up, new_down = staged(
            jnp.concatenate([tokens_one, tokens_two], axis=0),
            jnp.concatenate([experts_one, experts_two], axis=0),
            jnp.concatenate([gates_one, gates_two], axis=0),
            old_placement,
            gate_up,
            down,
            step,
            finish,
        )
        return (total[:count], total[count:], new_gate_up, new_down)
    slot_index = jnp.arange(peer_total, dtype=jnp.int32)
    old_slots = slot_table(old_placement, slot_index)
    joined_w = gate_up[0].reshape(gate_up.shape[1], -1)
    outs = []
    for tokens, chosen, gates in (
        (tokens_one, experts_one, gates_one),
        (tokens_two, experts_two, gates_two),
    ):
        rows = lax.all_gather(tokens, "tensor", axis=0, tiled=True)
        outs.append(routed_layer(rows, chosen, gates, old_slots, joined_w, down[0]))
    for items in PLAN:
        step(items, lambda: ())
    new_gate_up, new_down = finish()
    return (outs[0], outs[1], new_gate_up, new_down)


def solution(mesh):
    return jax.shard_map(
        body,
        mesh=mesh,
        in_specs=(
            P(("groups", "expert", "tensor"), None),
            P(("groups", "expert", "tensor"), None),
            P(("groups", "expert"), None),
            P(("groups", "expert"), None),
            P(("groups", "expert"), None),
            P(("groups", "expert"), None),
            P(),
            P(),
            P("expert", None, None, "tensor"),
            P("expert", "tensor", None),
        ),
        out_specs=(
            P(("groups", "expert", "tensor"), None),
            P(("groups", "expert", "tensor"), None),
            P(("groups", "expert"), None, None, "tensor"),
            P(("groups", "expert"), "tensor", None),
        ),
        check_vma=False,
    )
```

```python
import functools
import math

import jax
import jax.numpy as jnp
from jax import lax
from jax.experimental import pallas as pl
from jax.experimental.pallas import tpu as pltpu
from jax.sharding import PartitionSpec as P

LANES = 128


def xor_pairs(count, mask):
    return [(source, source ^ mask) for source in range(count)]


def shift_pairs(count, shift):
    return [(source, (source + shift) % count) for source in range(count)]


def exchange(value, mask):
    return lax.ppermute(value, "expert", xor_pairs(lax.axis_size("expert"), mask))


def slot_table(placement, slot_index):
    match_table = placement[:, None] == slot_index[None, :]
    return jnp.sum(jnp.where(match_table, slot_index[:, None], 0), axis=0)


def expert_ffn(rows, joined_w, down_w):
    half_width = down_w.shape[0]
    projected = jnp.dot(rows, joined_w, preferred_element_type=jnp.float32)
    hidden = (jax.nn.silu(projected[:, :half_width]) * projected[:, half_width:]).astype(
        jnp.bfloat16
    )
    return jnp.dot(hidden, down_w, preferred_element_type=jnp.float32)


def routed_layer(pair_rows, chosen, gates, slot_of, joined_w, down_w):
    row_total = pair_rows.shape[0]
    width = pair_rows.shape[1]
    top_count = chosen.shape[1]
    peer_total = lax.axis_size("expert")
    capacity = min(row_total, max(2, 3 * row_total * top_count // (2 * peer_total)))
    norm_gates = gates / jnp.sum(gates, axis=-1, keepdims=True)
    slot_index = jnp.arange(peer_total, dtype=jnp.int32)
    flat_ids = chosen.reshape(-1)
    expert_hot = flat_ids[:, None] == slot_index[None, :]
    target = jnp.sum(jnp.where(expert_hot, slot_of[None, :], 0), axis=1)
    target_hot = target[:, None] == slot_index[None, :]
    running = jnp.cumsum(target_hot.astype(jnp.int32), axis=0)
    position = jnp.sum(jnp.where(target_hot, running, 0), axis=1) - 1
    outgoing = jnp.zeros((peer_total, capacity, width), jnp.bfloat16)
    outgoing = outgoing.at[target, position].set(jnp.repeat(pair_rows, top_count, axis=0))
    received = lax.all_to_all(outgoing, "expert", split_axis=0, concat_axis=0, tiled=True)
    partial_rows = expert_ffn(received.reshape(-1, width), joined_w, down_w).astype(jnp.bfloat16)
    returned = lax.all_to_all(
        partial_rows.reshape(received.shape), "expert", split_axis=0, concat_axis=0, tiled=True
    )
    picked = returned[target, position].astype(jnp.float32)
    weighted = picked * norm_gates.reshape(-1)[:, None]
    partial_value = jnp.sum(weighted.reshape(row_total, top_count, width), axis=1)
    return lax.psum_scatter(partial_value, "tensor", scatter_dimension=0, tiled=True).astype(
        jnp.bfloat16
    )


def extended_rows(rows, chosen, gates, placement):
    norm_gates = gates / jnp.sum(gates, axis=-1, keepdims=True)
    hot = chosen[:, :, None] == placement[None, None, :]
    dense = jnp.sum(jnp.where(hot, norm_gates[:, :, None], 0.0), axis=1)
    high = lax.reduce_precision(dense, 8, 7)
    middle = lax.reduce_precision(dense - high, 8, 7)
    low = dense - high - middle
    slots = placement.shape[0]
    spare = jnp.zeros((rows.shape[0], LANES - 3 * slots), jnp.bfloat16)
    parts = [part.astype(jnp.bfloat16) for part in (high, middle, low)]
    return jnp.concatenate([rows, *parts, spare], axis=1)


def weighted_ffn(piece, width, slots, joined_w, down_w):
    own_index = lax.axis_index("expert")
    tail = piece[:, width:].astype(jnp.float32)
    column = lax.broadcasted_iota(jnp.int32, tail.shape, 1)
    mine = (column % slots == own_index) & (column < 3 * slots)
    weight = jnp.sum(jnp.where(mine, tail, 0.0), axis=1, keepdims=True)
    return weight * expert_ffn(piece[:, :width], joined_w, down_w)


def half_piece(array, half, index, count):
    rows = array.shape[1] // (2 * count)
    return lax.dynamic_slice_in_dim(array, (half * count + index) * rows, rows, axis=1)


def copies_kernel(places, group_ref, *refs):
    count = len(places)
    sources, outputs = refs[:count], refs[-4 - count : -2 - count]
    held, in_sems, out_sems = refs[-2 - count : -2], refs[-2], refs[-1]
    group = group_ref[0]
    inward, outward = [], []
    for number, (source, place) in enumerate(zip(sources, places)):
        if len(place) == 5:
            output, mine, first, span, rows = place
            half = group if mine else 1 - group
            start = pl.multiple_of(half * span + first, 16)
        else:
            output, start, rows = place
            source = source.at[:, pl.ds(start, rows)]
        target = outputs[output].at[:, pl.ds(start, rows)]
        inward.append(pltpu.make_async_copy(source, held[number], in_sems.at[number]))
        outward.append(pltpu.make_async_copy(held[number], target, out_sems.at[number]))
    for copy in inward:
        copy.start()
    for arrival, departure in zip(inward, outward):
        arrival.wait()
        departure.start()
    for departure in outward:
        departure.wait()


def place_pieces(group, sources, places, likes, onto=None):
    count = len(sources)
    anywhere = pl.BlockSpec(memory_space=pl.ANY)
    extra = list(onto) if onto is not None else []
    held = [
        pltpu.VMEM((source.shape[0], place[-1], *source.shape[2:]), source.dtype)
        for source, place in zip(sources, places)
    ]
    moved = sum(math.prod(one.shape) * one.dtype.itemsize for one in held)
    return pl.pallas_call(
        functools.partial(copies_kernel, places),
        out_shape=[jax.ShapeDtypeStruct(like.shape, like.dtype) for like in likes],
        in_specs=[pl.BlockSpec(memory_space=pltpu.SMEM)] + [anywhere] * (count + len(extra)),
        out_specs=[anywhere] * len(likes),
        scratch_shapes=[
            *held,
            pltpu.SemaphoreType.DMA((count,)),
            pltpu.SemaphoreType.DMA((count,)),
        ],
        input_output_aliases={1 + count + k: k for k in range(len(extra))},
        cost_estimate=pl.CostEstimate(flops=0, bytes_accessed=2 * moved, transcendentals=0),
        compiler_params=pltpu.CompilerParams(vmem_limit_bytes=moved + (4 << 20)),
    )(group.reshape(1), *sources, *extra)


PLAN = (
    (("g", 0),),
    (("g", 1), ("d", 0)),
    (("g", 2),),
    (("g", 3), ("d", 1)),
)
COUNTS = {
    name: sum(1 for items in PLAN for kind, _ in items if kind == name) for name in ("g", "d")
}
GROUP_PAIRS = [(0, 1), (1, 0)]


class Swap:
    def __init__(self, on, group, gate_up, down):
        self.on, self.group = on, group
        self.source = {"g": gate_up, "d": down}
        self.half_bit = lax.axis_size("expert") // 2
        self.arrived, self.relayed, self.pending = {}, {}, ()
        self.ready = self.cut(PLAN[0])

    def cut(self, items):
        return [half_piece(self.source[n], self.group, k, COUNTS[n]) for n, k in items]

    def step(self, turn, work):
        items = PLAN[turn]
        outgoing = self.ready
        to_relay = [self.arrived[item] for item in self.pending]
        following = PLAN[turn + 1] if turn + 1 < len(PLAN) else ()

        def active(args):
            outgoing, to_relay = args
            crossed = [exchange(value, self.half_bit) for value in outgoing]
            handed = [lax.ppermute(value, "groups", GROUP_PAIRS) for value in to_relay]
            return crossed, handed, lax.optimization_barrier((self.cut(following), work()))

        def idle(args):
            outgoing, to_relay = args
            return list(outgoing), list(to_relay), ([*self.cut(following)], work())

        crossed, handed, (self.ready, made) = lax.cond(self.on, active, idle, (outgoing, to_relay))
        self.relayed.update(zip(self.pending, handed))
        self.arrived.update(zip(items, crossed))
        self.pending = items
        return made

    def place(self, item, mine):
        name, index = item
        rows = self.source[name].shape[1]
        size = rows // (2 * COUNTS[name])
        return (0 if name == "g" else 1, mine, index * size, rows // 2, size)

    def finish(self):
        likes = (self.source["g"], self.source["d"])
        last = self.pending
        to_relay = [self.arrived[item] for item in last]

        def active(to_relay):
            handed = [lax.ppermute(value, "groups", GROUP_PAIRS) for value in to_relay]
            sources = list(self.arrived.values()) + list(self.relayed.values())
            places = [self.place(item, True) for item in self.arrived]
            places += [self.place(item, False) for item in self.relayed]
            partial_pair = place_pieces(self.group, sources, places, likes)
            return tuple(
                place_pieces(
                    self.group, handed, [self.place(item, False) for item in last], likes, partial_pair
                )
            )

        def idle(_):
            places = []
            for output, like in enumerate(likes):
                rows = like.shape[1] // 4
                places += [(output, index * rows, rows) for index in range(4)]
            return tuple(place_pieces(self.group, [likes[p[0]] for p in places], places, likes))

        return lax.cond(self.on, active, idle, to_relay)


def staged(tokens, chosen, gates, placement, gate_up, down, swap):
    peers = lax.axis_size("expert")
    levels = peers // 4
    rows, width = tokens.shape
    own = extended_rows(tokens, chosen, gates, placement)

    def ffn(first, second, joined_w):
        piece = jnp.concatenate([first, second], axis=0)
        part = weighted_ffn(piece, width, peers, joined_w, down[0])
        count = first.shape[0]
        return part[:count], part[count:].astype(jnp.bfloat16)

    columns = [own] + [
        lax.ppermute(own, "expert", shift_pairs(peers, 4 * hop)) for hop in range(1, levels)
    ]
    joined_w = swap.step(0, lambda: gate_up[0].reshape(width, -1))
    columns, joined_w = lax.optimization_barrier((columns, joined_w))
    here = jnp.concatenate(columns, axis=0)
    here_core = exchange(here, 1)
    across = exchange(here, 2)
    part_here, part_here_core = swap.step(1, lambda: ffn(here, here_core, joined_w))
    across, part_here_core = lax.optimization_barrier((across, part_here_core))
    across_core = exchange(across, 1)
    got_here = exchange(part_here_core, 1)
    part_across, part_across_core = swap.step(2, lambda: ffn(across, across_core, joined_w))
    got_across = exchange(part_across_core, 1)
    sum_across = (part_across + got_across.astype(jnp.float32)).astype(jnp.bfloat16)
    got_column = exchange(sum_across, 2)
    sum_here = swap.step(3, lambda: part_here + got_here.astype(jnp.float32))
    column = sum_here + got_column.astype(jnp.float32)
    total = column[:rows]
    returned = [
        lax.ppermute(
            column[hop * rows : (hop + 1) * rows].astype(jnp.bfloat16),
            "expert",
            shift_pairs(peers, peers - 4 * hop),
        )
        for hop in range(1, levels)
    ]
    new_gate_up, new_down = swap.finish()
    for value in returned:
        total = total + value.astype(jnp.float32)
    total = total.astype(jnp.bfloat16)
    return total, new_gate_up, new_down


def body(
    tokens_one,
    tokens_two,
    experts_one,
    experts_two,
    gates_one,
    gates_two,
    old_placement,
    swap_flags,
    gate_up,
    down,
):
    peer_total = lax.axis_size("expert")
    half_count = peer_total // 2
    own_index = lax.axis_index("expert")
    group = lax.axis_index("groups")
    swap_here = swap_flags[own_index % half_count] == 1
    swap = Swap(swap_here, group, gate_up, down)
    if lax.axis_size("tensor") == 1 and peer_total == 16:
        count = tokens_one.shape[0]
        total, new_gate_up, new_down = staged(
            jnp.concatenate([tokens_one, tokens_two], axis=0),
            jnp.concatenate([experts_one, experts_two], axis=0),
            jnp.concatenate([gates_one, gates_two], axis=0),
            old_placement,
            gate_up,
            down,
            swap,
        )
        return (total[:count], total[count:], new_gate_up, new_down)
    slot_index = jnp.arange(peer_total, dtype=jnp.int32)
    old_slots = slot_table(old_placement, slot_index)
    joined_w = gate_up[0].reshape(gate_up.shape[1], -1)
    outs = []
    for tokens, chosen, gates in (
        (tokens_one, experts_one, gates_one),
        (tokens_two, experts_two, gates_two),
    ):
        rows = lax.all_gather(tokens, "tensor", axis=0, tiled=True)
        outs.append(routed_layer(rows, chosen, gates, old_slots, joined_w, down[0]))
    for turn in range(len(PLAN)):
        swap.step(turn, lambda: ())
    new_gate_up, new_down = swap.finish()
    return (outs[0], outs[1], new_gate_up, new_down)


def solution(mesh):
    return jax.shard_map(
        body,
        mesh=mesh,
        in_specs=(
            P(("groups", "expert", "tensor"), None),
            P(("groups", "expert", "tensor"), None),
            P(("groups", "expert"), None),
            P(("groups", "expert"), None),
            P(("groups", "expert"), None),
            P(("groups", "expert"), None),
            P(),
            P(),
            P("expert", None, None, "tensor"),
            P("expert", "tensor", None),
        ),
        out_specs=(
            P(("groups", "expert", "tensor"), None),
            P(("groups", "expert", "tensor"), None),
            P(("groups", "expert"), None, None, "tensor"),
            P(("groups", "expert"), "tensor", None),
        ),
        check_vma=False,
    )
```

```python
import functools
import math

import jax
import jax.numpy as jnp
from jax import lax
from jax.experimental import pallas as pl
from jax.experimental.pallas import tpu as pltpu
from jax.sharding import PartitionSpec as P

LANES = 128


def xor_pairs(count, mask):
    return [(source, source ^ mask) for source in range(count)]


def shift_pairs(count, shift):
    return [(source, (source + shift) % count) for source in range(count)]


def exchange(value, mask):
    return lax.ppermute(value, "expert", xor_pairs(lax.axis_size("expert"), mask))


def slot_table(placement, slot_index):
    match_table = placement[:, None] == slot_index[None, :]
    return jnp.sum(jnp.where(match_table, slot_index[:, None], 0), axis=0)


def expert_ffn(rows, joined_w, down_w):
    half_width = down_w.shape[0]
    projected = jnp.dot(rows, joined_w, preferred_element_type=jnp.float32)
    hidden = (jax.nn.silu(projected[:, :half_width]) * projected[:, half_width:]).astype(
        jnp.bfloat16
    )
    return jnp.dot(hidden, down_w, preferred_element_type=jnp.float32)


def routed_layer(pair_rows, chosen, gates, slot_of, joined_w, down_w):
    row_total = pair_rows.shape[0]
    width = pair_rows.shape[1]
    top_count = chosen.shape[1]
    peer_total = lax.axis_size("expert")
    capacity = min(row_total, max(2, 3 * row_total * top_count // (2 * peer_total)))
    norm_gates = gates / jnp.sum(gates, axis=-1, keepdims=True)
    slot_index = jnp.arange(peer_total, dtype=jnp.int32)
    flat_ids = chosen.reshape(-1)
    expert_hot = flat_ids[:, None] == slot_index[None, :]
    target = jnp.sum(jnp.where(expert_hot, slot_of[None, :], 0), axis=1)
    target_hot = target[:, None] == slot_index[None, :]
    running = jnp.cumsum(target_hot.astype(jnp.int32), axis=0)
    position = jnp.sum(jnp.where(target_hot, running, 0), axis=1) - 1
    outgoing = jnp.zeros((peer_total, capacity, width), jnp.bfloat16)
    outgoing = outgoing.at[target, position].set(jnp.repeat(pair_rows, top_count, axis=0))
    received = lax.all_to_all(outgoing, "expert", split_axis=0, concat_axis=0, tiled=True)
    partial_rows = expert_ffn(received.reshape(-1, width), joined_w, down_w).astype(jnp.bfloat16)
    returned = lax.all_to_all(
        partial_rows.reshape(received.shape), "expert", split_axis=0, concat_axis=0, tiled=True
    )
    picked = returned[target, position].astype(jnp.float32)
    weighted = picked * norm_gates.reshape(-1)[:, None]
    partial_value = jnp.sum(weighted.reshape(row_total, top_count, width), axis=1)
    return lax.psum_scatter(partial_value, "tensor", scatter_dimension=0, tiled=True).astype(
        jnp.bfloat16
    )


def extended_rows(rows, chosen, gates, placement):
    norm_gates = gates / jnp.sum(gates, axis=-1, keepdims=True)
    hot = chosen[:, :, None] == placement[None, None, :]
    dense = jnp.sum(jnp.where(hot, norm_gates[:, :, None], 0.0), axis=1)
    high = lax.reduce_precision(dense, 8, 7)
    middle = lax.reduce_precision(dense - high, 8, 7)
    low = dense - high - middle
    slots = placement.shape[0]
    spare = jnp.zeros((rows.shape[0], LANES - 3 * slots), jnp.bfloat16)
    parts = [part.astype(jnp.bfloat16) for part in (high, middle, low)]
    return jnp.concatenate([rows, *parts, spare], axis=1)


def ffn_kernel(slots, own_ref, first_ref, second_ref, gate_ref, up_ref, down_ref, near_ref, far_ref, total):
    turn, turns = pl.program_id(0), pl.num_programs(0)
    width = near_ref.shape[1]

    for number, (rows_ref, out_ref) in enumerate(((first_ref, near_ref), (second_ref, far_ref))):
        rows = rows_ref[:, :width]
        gate = jnp.dot(rows, gate_ref[...], preferred_element_type=jnp.float32)
        up = jnp.dot(rows, up_ref[...], preferred_element_type=jnp.float32)
        hidden = (jax.nn.silu(gate) * up).astype(jnp.bfloat16)
        part = jnp.dot(hidden, down_ref[...], preferred_element_type=jnp.float32)

        @pl.when(turn == 0)
        def _(number=number, part=part):
            total[number] = part

        @pl.when(turn > 0)
        def _(number=number, part=part):
            total[number] += part

        @pl.when(turn == turns - 1)
        def _(number=number, rows_ref=rows_ref, out_ref=out_ref):
            tail = rows_ref[:, width:].astype(jnp.float32)
            column = lax.broadcasted_iota(jnp.int32, tail.shape, 1)
            own = own_ref[0]
            mine = (column == own) | (column == own + slots) | (column == own + 2 * slots)
            weight = jnp.sum(jnp.where(mine, tail, 0.0), axis=1, keepdims=True)
            out_ref[...] = (weight * total[number]).astype(out_ref.dtype)


def weighted_ffn(first, second, slots, joined_w, down_w):
    rows, span = first.shape
    half_width, width = down_w.shape
    tile = 256
    tiles = half_width // tile
    own = lax.axis_index("expert").astype(jnp.int32).reshape(1)
    whole = pl.BlockSpec((rows, span), lambda turn: (0, 0))
    result = pl.BlockSpec((rows, width), lambda turn: (0, 0))
    return pl.pallas_call(
        functools.partial(ffn_kernel, slots),
        grid=(tiles,),
        in_specs=[
            pl.BlockSpec(memory_space=pltpu.SMEM),
            whole,
            whole,
            pl.BlockSpec((width, tile), lambda turn: (0, turn)),
            pl.BlockSpec((width, tile), lambda turn: (0, tiles + turn)),
            pl.BlockSpec((tile, width), lambda turn: (turn, 0)),
        ],
        out_specs=[result, result],
        out_shape=[
            jax.ShapeDtypeStruct((rows, width), jnp.float32),
            jax.ShapeDtypeStruct((rows, width), jnp.bfloat16),
        ],
        scratch_shapes=[pltpu.VMEM((2, rows, width), jnp.float32)],
        cost_estimate=pl.CostEstimate(
            flops=12 * rows * width * half_width,
            bytes_accessed=6 * width * half_width + 10 * rows * width,
            transcendentals=2 * rows * half_width,
        ),
        compiler_params=pltpu.CompilerParams(vmem_limit_bytes=26 << 20),
    )(own, first, second, joined_w, joined_w, down_w)


def copies_kernel(places, swaps, owns, numbers_ref, *refs):
    count = len(places)
    pieces = refs[: count if swaps else 0]
    own_refs = refs[len(pieces) : len(pieces) + 2]
    outputs, held = refs[-4 - count : -2 - count], refs[-2 - count : -2]
    in_sems, out_sems = refs[-2], refs[-1]
    group, on = numbers_ref[0], numbers_ref[1]

    def cut(refs, place):
        output, mine, first, span, rows = place
        half = group if mine else 1 - group
        start = pl.multiple_of(half * span + first, 16)
        return refs[output].at[:, pl.ds(start, rows)]

    def run(sources):
        inward = [
            pltpu.make_async_copy(source, held[k], in_sems.at[k]) for k, source in enumerate(sources)
        ]
        outward = [
            pltpu.make_async_copy(held[k], cut(outputs, place), out_sems.at[k])
            for k, place in enumerate(places)
        ]
        for copy in inward:
            copy.start()
        for arrival, departure in zip(inward, outward):
            arrival.wait()
            departure.start()
        for departure in outward:
            departure.wait()

    if swaps and owns:
        pl.when(on == 1)(lambda: run(pieces))
        pl.when(on == 0)(lambda: run([cut(own_refs, place) for place in places]))
    elif swaps:
        run(pieces)
    else:
        run([cut(own_refs, place) for place in places])


def place_pieces(numbers, sources, places, likes, owns=False, onto=None):
    anywhere = pl.BlockSpec(memory_space=pl.ANY)
    extra = list(onto) if onto is not None else []
    given = list(sources) + (list(likes) if owns else [])
    held = []
    for output, _, _, _, rows in places:
        like = likes[output]
        held.append(pltpu.VMEM((like.shape[0], rows, *like.shape[2:]), like.dtype))
    moved = sum(math.prod(one.shape) * one.dtype.itemsize for one in held)
    return pl.pallas_call(
        functools.partial(copies_kernel, places, len(sources) > 0, owns),
        out_shape=[jax.ShapeDtypeStruct(like.shape, like.dtype) for like in likes],
        in_specs=[pl.BlockSpec(memory_space=pltpu.SMEM)] + [anywhere] * (len(given) + len(extra)),
        out_specs=[anywhere] * len(likes),
        scratch_shapes=[
            *held,
            pltpu.SemaphoreType.DMA((len(held),)),
            pltpu.SemaphoreType.DMA((len(held),)),
        ],
        input_output_aliases={1 + len(given) + k: k for k in range(len(extra))},
        cost_estimate=pl.CostEstimate(flops=0, bytes_accessed=2 * moved, transcendentals=0),
        compiler_params=pltpu.CompilerParams(vmem_limit_bytes=moved + (2 << 20)),
    )(numbers, *given, *extra)


UNITS = {"g": 8, "d": 4}
PLAN = (
    (("g", 0, 2), ("g", 2, 2)),
    (("d", 0, 2), ("g", 4, 2)),
    (("d", 2, 1), ("g", 6, 1)),
    (("d", 3, 1), ("g", 7, 1)),
)
AT_ONCE = (0, 0, 0, 0)
GROUP_PAIRS = [(0, 1), (1, 0)]


class Swap:
    def __init__(self, flags, gate_up, down):
        peers = lax.axis_size("expert")
        self.peers, self.half = peers, peers // 2
        self.group = lax.axis_index("groups")
        self.source = {"g": gate_up, "d": down}
        self.on = flags[lax.axis_index("expert") % self.half] == 1
        self.numbers = jnp.stack([self.group.astype(jnp.int32), self.on.astype(jnp.int32)])
        self.arrived, self.relayed, self.waiting = {}, {}, ()
        self.ready = [self.cut(item) for item in PLAN[0]]

    def unit(self, name):
        return self.source[name].shape[1] // (2 * UNITS[name])

    def cut(self, item):
        name, first, units = item
        unit = self.unit(name)
        start = (self.group * UNITS[name] + first) * unit
        return lax.dynamic_slice_in_dim(self.source[name], start, units * unit, axis=1)

    def hand(self, value):
        return lax.ppermute(value, "groups", GROUP_PAIRS)

    def step(self, turn, work):
        items = PLAN[turn]
        direct = AT_ONCE[turn]
        handing = (*self.waiting, *items[:direct])
        held = [self.arrived[item] for item in self.waiting]

        following = PLAN[turn + 1] if turn + 1 < len(PLAN) else ()

        def active(args):
            outgoing, held = args
            crossed = [exchange(value, self.half) for value in outgoing]
            handed = [self.hand(value) for value in held]
            handed += [self.hand(value) for value in crossed[:direct]]
            ready = [self.cut(item) for item in following]
            return crossed, handed, *lax.optimization_barrier((ready, work()))

        def idle(_):
            empty = {}
            for name, first, units in (*items, *handing, *following):
                shape = list(self.source[name].shape)
                shape[1] = self.unit(name) * units
                empty[name, first, units] = jnp.zeros(shape, jnp.bfloat16)
            some = [[empty[item] for item in group] for group in (items, handing, following)]
            return *some, work()

        crossed, handed, self.ready, made = lax.cond(self.on, active, idle, (self.ready, held))
        self.relayed.update(zip(handing, handed))
        self.arrived.update(zip(items, crossed))
        self.waiting = items[direct:]
        return made

    def place(self, item, mine):
        name, first, units = item
        rows = self.source[name].shape[1]
        unit = self.unit(name)
        return (0 if name == "g" else 1, mine, first * unit, rows // 2, units * unit)

    def finish(self):
        likes = (self.source["g"], self.source["d"])
        held = [self.arrived[item] for item in self.waiting]
        early = [self.place(item, True) for item in self.arrived]
        early += [self.place(item, False) for item in self.relayed]
        late = [self.place(item, False) for item in self.waiting]

        def active(held):
            handed = [self.hand(value) for value in held]
            sources = list(self.arrived.values()) + list(self.relayed.values())
            begun = place_pieces(self.numbers, sources, early, likes)
            return tuple(place_pieces(self.numbers, handed, late, likes, onto=begun))

        def idle(_):
            return tuple(place_pieces(self.numbers, [], early + late, likes, True))

        return lax.cond(self.on, active, idle, held)


def staged(tokens, chosen, gates, placement, gate_up, down, swap):
    peers = lax.axis_size("expert")
    levels = peers // 4
    rows, width = tokens.shape
    own = extended_rows(tokens, chosen, gates, placement)

    def ffn(first, second, joined_w):
        return weighted_ffn(first, second, peers, joined_w, down[0])

    columns = [own] + [
        lax.ppermute(own, "expert", shift_pairs(peers, 4 * hop)) for hop in range(1, levels)
    ]
    joined_w = swap.step(0, lambda: gate_up[0].reshape(width, -1))
    columns, joined_w = lax.optimization_barrier((columns, joined_w))
    here = jnp.concatenate(columns, axis=0)
    here_core = exchange(here, 1)
    across = exchange(here, 2)
    part_here, part_here_core = swap.step(1, lambda: ffn(here, here_core, joined_w))
    across, part_here_core = lax.optimization_barrier((across, part_here_core))
    across_core = exchange(across, 1)
    got_here = exchange(part_here_core, 1)
    part_across, part_across_core = swap.step(2, lambda: ffn(across, across_core, joined_w))
    got_across = exchange(part_across_core, 1)
    sum_across = (part_across + got_across.astype(jnp.float32)).astype(jnp.bfloat16)
    got_column = exchange(sum_across, 2)
    sum_here = swap.step(3, lambda: part_here + got_here.astype(jnp.float32))
    column = sum_here + got_column.astype(jnp.float32)
    total = column[:rows]
    returned = [
        lax.ppermute(
            column[hop * rows : (hop + 1) * rows].astype(jnp.bfloat16),
            "expert",
            shift_pairs(peers, peers - 4 * hop),
        )
        for hop in range(1, levels)
    ]
    new_gate_up, new_down = swap.finish()
    for value in returned:
        total = total + value.astype(jnp.float32)
    total = total.astype(jnp.bfloat16)
    return total, new_gate_up, new_down


def body(
    tokens_one,
    tokens_two,
    experts_one,
    experts_two,
    gates_one,
    gates_two,
    old_placement,
    swap_flags,
    gate_up,
    down,
):
    peer_total = lax.axis_size("expert")
    swap = Swap(swap_flags, gate_up, down)
    if lax.axis_size("tensor") == 1 and peer_total == 16:
        count = tokens_one.shape[0]
        total, new_gate_up, new_down = staged(
            jnp.concatenate([tokens_one, tokens_two], axis=0),
            jnp.concatenate([experts_one, experts_two], axis=0),
            jnp.concatenate([gates_one, gates_two], axis=0),
            old_placement,
            gate_up,
            down,
            swap,
        )
        return (total[:count], total[count:], new_gate_up, new_down)
    slot_index = jnp.arange(peer_total, dtype=jnp.int32)
    old_slots = slot_table(old_placement, slot_index)
    joined_w = gate_up[0].reshape(gate_up.shape[1], -1)
    outs = []
    for tokens, chosen, gates in (
        (tokens_one, experts_one, gates_one),
        (tokens_two, experts_two, gates_two),
    ):
        rows = lax.all_gather(tokens, "tensor", axis=0, tiled=True)
        outs.append(routed_layer(rows, chosen, gates, old_slots, joined_w, down[0]))
    for turn in range(len(PLAN)):
        swap.step(turn, lambda: ())
    new_gate_up, new_down = swap.finish()
    return (outs[0], outs[1], new_gate_up, new_down)


def solution(mesh):
    return jax.shard_map(
        body,
        mesh=mesh,
        in_specs=(
            P(("groups", "expert", "tensor"), None),
            P(("groups", "expert", "tensor"), None),
            P(("groups", "expert"), None),
            P(("groups", "expert"), None),
            P(("groups", "expert"), None),
            P(("groups", "expert"), None),
            P(),
            P(),
            P("expert", None, None, "tensor"),
            P("expert", "tensor", None),
        ),
        out_specs=(
            P(("groups", "expert", "tensor"), None),
            P(("groups", "expert", "tensor"), None),
            P(("groups", "expert"), None, None, "tensor"),
            P(("groups", "expert"), "tensor", None),
        ),
        check_vma=False,
    )
```

```python
import functools
import math

import jax
import jax.numpy as jnp
from jax import lax
from jax.experimental import pallas as pl
from jax.experimental.pallas import tpu as pltpu
from jax.sharding import PartitionSpec as P

LANES = 128


def xor_pairs(count, mask):
    return [(source, source ^ mask) for source in range(count)]


def shift_pairs(count, shift):
    return [(source, (source + shift) % count) for source in range(count)]


def exchange(value, mask):
    return lax.ppermute(value, "expert", xor_pairs(lax.axis_size("expert"), mask))


def slot_table(placement, slot_index):
    match_table = placement[:, None] == slot_index[None, :]
    return jnp.sum(jnp.where(match_table, slot_index[:, None], 0), axis=0)


def expert_ffn(rows, joined_w, down_w):
    half_width = down_w.shape[0]
    projected = jnp.dot(rows, joined_w, preferred_element_type=jnp.float32)
    hidden = (jax.nn.silu(projected[:, :half_width]) * projected[:, half_width:]).astype(
        jnp.bfloat16
    )
    return jnp.dot(hidden, down_w, preferred_element_type=jnp.float32)


def routed_layer(pair_rows, chosen, gates, slot_of, joined_w, down_w):
    row_total = pair_rows.shape[0]
    width = pair_rows.shape[1]
    top_count = chosen.shape[1]
    peer_total = lax.axis_size("expert")
    capacity = min(row_total, max(2, 3 * row_total * top_count // (2 * peer_total)))
    norm_gates = gates / jnp.sum(gates, axis=-1, keepdims=True)
    slot_index = jnp.arange(peer_total, dtype=jnp.int32)
    flat_ids = chosen.reshape(-1)
    expert_hot = flat_ids[:, None] == slot_index[None, :]
    target = jnp.sum(jnp.where(expert_hot, slot_of[None, :], 0), axis=1)
    target_hot = target[:, None] == slot_index[None, :]
    running = jnp.cumsum(target_hot.astype(jnp.int32), axis=0)
    position = jnp.sum(jnp.where(target_hot, running, 0), axis=1) - 1
    outgoing = jnp.zeros((peer_total, capacity, width), jnp.bfloat16)
    outgoing = outgoing.at[target, position].set(jnp.repeat(pair_rows, top_count, axis=0))
    received = lax.all_to_all(outgoing, "expert", split_axis=0, concat_axis=0, tiled=True)
    partial_rows = expert_ffn(received.reshape(-1, width), joined_w, down_w).astype(jnp.bfloat16)
    returned = lax.all_to_all(
        partial_rows.reshape(received.shape), "expert", split_axis=0, concat_axis=0, tiled=True
    )
    picked = returned[target, position].astype(jnp.float32)
    weighted = picked * norm_gates.reshape(-1)[:, None]
    partial_value = jnp.sum(weighted.reshape(row_total, top_count, width), axis=1)
    return lax.psum_scatter(partial_value, "tensor", scatter_dimension=0, tiled=True).astype(
        jnp.bfloat16
    )


def extended_kernel(placement_ref, *refs):
    out_ref = refs[-1]
    slots = placement_ref.shape[0]
    parts = (len(refs) - 1) // 3
    for number in range(parts):
        rows_ref, chosen_ref, gates_ref = refs[3 * number : 3 * number + 3]
        rows, width = rows_ref.shape
        chosen, gates = chosen_ref[...], gates_ref[...]
        weights = gates / jnp.sum(gates, axis=0, keepdims=True)
        slot = lax.broadcasted_iota(jnp.int32, (slots, rows), 0)
        dense = jnp.zeros((slots, rows), jnp.float32)
        for index in range(slots):
            named = jnp.where(chosen == placement_ref[index], weights, 0.0)
            dense = jnp.where(slot == index, jnp.sum(named, axis=0, keepdims=True), dense)
        tail = jnp.zeros((rows, LANES), jnp.float32)
        for place in range(3):
            part = dense.astype(jnp.bfloat16)
            dense = dense - part.astype(jnp.float32)
            lane = lax.broadcasted_iota(jnp.int32, (slots, LANES), 1)
            row = lax.broadcasted_iota(jnp.int32, (slots, LANES), 0)
            spot = (lane == row + place * slots).astype(jnp.float32).astype(jnp.bfloat16)
            tail += lax.dot_general(
                part, spot, (((0,), (0,)), ((), ())), preferred_element_type=jnp.float32
            )
        out_ref[number * rows : (number + 1) * rows, :width] = rows_ref[...]
        out_ref[number * rows : (number + 1) * rows, width:] = tail.astype(jnp.bfloat16)


def extended_rows(batches, placement):
    rows, width = batches[0][0].shape
    vmem = pl.BlockSpec(memory_space=pltpu.VMEM)
    given = [array for tokens, chosen, gates in batches for array in (tokens, chosen.T, gates.T)]
    return pl.pallas_call(
        extended_kernel,
        out_shape=jax.ShapeDtypeStruct((len(batches) * rows, width + LANES), jnp.bfloat16),
        in_specs=[pl.BlockSpec(memory_space=pltpu.SMEM)] + [vmem] * len(given),
        out_specs=vmem,
    )(placement, *given)


def ffn_kernel(slots, own_ref, first_ref, second_ref, gate_ref, up_ref, down_ref, near_ref, far_ref, total):
    turn, turns = pl.program_id(0), pl.num_programs(0)
    width = near_ref.shape[1]

    for number, (rows_ref, out_ref) in enumerate(((first_ref, near_ref), (second_ref, far_ref))):
        rows = rows_ref[:, :width]
        gate = jnp.dot(rows, gate_ref[...], preferred_element_type=jnp.float32)
        up = jnp.dot(rows, up_ref[...], preferred_element_type=jnp.float32)
        hidden = (jax.nn.silu(gate) * up).astype(jnp.bfloat16)
        part = jnp.dot(hidden, down_ref[...], preferred_element_type=jnp.float32)

        @pl.when(turn == 0)
        def _(number=number, part=part):
            total[number] = part

        @pl.when(turn > 0)
        def _(number=number, part=part):
            total[number] += part

        @pl.when(turn == turns - 1)
        def _(number=number, rows_ref=rows_ref, out_ref=out_ref):
            tail = rows_ref[:, width:].astype(jnp.float32)
            column = lax.broadcasted_iota(jnp.int32, tail.shape, 1)
            own = own_ref[0]
            mine = (column == own) | (column == own + slots) | (column == own + 2 * slots)
            weight = jnp.sum(jnp.where(mine, tail, 0.0), axis=1, keepdims=True)
            out_ref[...] = (weight * total[number]).astype(out_ref.dtype)


def weighted_ffn(first, second, slots, joined_w, down_w):
    rows, span = first.shape
    half_width, width = down_w.shape
    tile = 256
    tiles = half_width // tile
    own = lax.axis_index("expert").astype(jnp.int32).reshape(1)
    once = pl.Buffered(1)
    whole = pl.BlockSpec((rows, span), lambda turn: (0, 0), pipeline_mode=once)
    result = pl.BlockSpec((rows, width), lambda turn: (0, 0), pipeline_mode=once)
    return pl.pallas_call(
        functools.partial(ffn_kernel, slots),
        grid=(tiles,),
        in_specs=[
            pl.BlockSpec(memory_space=pltpu.SMEM),
            whole,
            whole,
            pl.BlockSpec((width, tile), lambda turn: (0, turn)),
            pl.BlockSpec((width, tile), lambda turn: (0, tiles + turn)),
            pl.BlockSpec((tile, width), lambda turn: (turn, 0)),
        ],
        out_specs=[result, result],
        out_shape=[
            jax.ShapeDtypeStruct((rows, width), jnp.float32),
            jax.ShapeDtypeStruct((rows, width), jnp.bfloat16),
        ],
        scratch_shapes=[pltpu.VMEM((2, rows, width), jnp.float32)],
        cost_estimate=pl.CostEstimate(
            flops=12 * rows * width * half_width,
            bytes_accessed=6 * width * half_width + 10 * rows * width,
            transcendentals=2 * rows * half_width,
        ),
        compiler_params=pltpu.CompilerParams(vmem_limit_bytes=21 << 20),
    )(own, first, second, joined_w, joined_w, down_w)


def copies_kernel(places, swaps, owns, numbers_ref, *refs):
    count = len(places)
    pieces = refs[: count if swaps else 0]
    own_refs = refs[len(pieces) : len(pieces) + 2]
    outputs, held = refs[-4 - count : -2 - count], refs[-2 - count : -2]
    in_sems, out_sems = refs[-2], refs[-1]
    group, on = numbers_ref[0], numbers_ref[1]

    def cut(refs, place):
        output, mine, first, span, rows = place
        half = group if mine else 1 - group
        start = pl.multiple_of(half * span + first, 16)
        return refs[output].at[:, pl.ds(start, rows)]

    def run(sources):
        inward = [
            pltpu.make_async_copy(source, held[k], in_sems.at[k]) for k, source in enumerate(sources)
        ]
        outward = [
            pltpu.make_async_copy(held[k], cut(outputs, place), out_sems.at[k])
            for k, place in enumerate(places)
        ]
        for copy in inward:
            copy.start()
        for arrival, departure in zip(inward, outward):
            arrival.wait()
            departure.start()
        for departure in outward:
            departure.wait()

    if swaps and owns:
        pl.when(on == 1)(lambda: run(pieces))
        pl.when(on == 0)(lambda: run([cut(own_refs, place) for place in places]))
    elif swaps:
        run(pieces)
    else:
        run([cut(own_refs, place) for place in places])


def place_pieces(numbers, sources, places, likes, owns=False, onto=None):
    anywhere = pl.BlockSpec(memory_space=pl.ANY)
    extra = list(onto) if onto is not None else []
    given = list(sources) + (list(likes) if owns else [])
    held = []
    for output, _, _, _, rows in places:
        like = likes[output]
        held.append(pltpu.VMEM((like.shape[0], rows, *like.shape[2:]), like.dtype))
    moved = sum(math.prod(one.shape) * one.dtype.itemsize for one in held)
    return pl.pallas_call(
        functools.partial(copies_kernel, places, len(sources) > 0, owns),
        out_shape=[jax.ShapeDtypeStruct(like.shape, like.dtype) for like in likes],
        in_specs=[pl.BlockSpec(memory_space=pltpu.SMEM)] + [anywhere] * (len(given) + len(extra)),
        out_specs=[anywhere] * len(likes),
        scratch_shapes=[
            *held,
            pltpu.SemaphoreType.DMA((len(held),)),
            pltpu.SemaphoreType.DMA((len(held),)),
        ],
        input_output_aliases={1 + len(given) + k: k for k in range(len(extra))},
        cost_estimate=pl.CostEstimate(flops=0, bytes_accessed=2 * moved, transcendentals=0),
        compiler_params=pltpu.CompilerParams(vmem_limit_bytes=moved + (2 << 20)),
    )(numbers, *given, *extra)


UNITS = {"g": 8, "d": 4}
PLAN = (
    (("g", 0, 2), ("g", 2, 2)),
    (("d", 0, 1), ("g", 4, 2)),
    (("d", 1, 1), ("d", 2, 1)),
    (("d", 3, 1), ("g", 6, 2)),
)
AT_ONCE = (0, 0, 0, 0)
GROUP_PAIRS = [(0, 1), (1, 0)]


class Swap:
    def __init__(self, flags, gate_up, down):
        peers = lax.axis_size("expert")
        self.peers, self.half = peers, peers // 2
        self.group = lax.axis_index("groups")
        self.source = {"g": gate_up, "d": down}
        self.on = flags[lax.axis_index("expert") % self.half] == 1
        self.numbers = jnp.stack([self.group.astype(jnp.int32), self.on.astype(jnp.int32)])
        self.arrived, self.relayed, self.waiting = {}, {}, ()
        self.ready = [self.cut(item) for item in PLAN[0]]

    def unit(self, name):
        return self.source[name].shape[1] // (2 * UNITS[name])

    def cut(self, item):
        name, first, units = item
        unit = self.unit(name)
        start = (self.group * UNITS[name] + first) * unit
        return lax.dynamic_slice_in_dim(self.source[name], start, units * unit, axis=1)

    def hand(self, value):
        return lax.ppermute(value, "groups", GROUP_PAIRS)

    def step(self, turn, work):
        items = PLAN[turn]
        direct = AT_ONCE[turn]
        handing = (*self.waiting, *items[:direct])
        held = [self.arrived[item] for item in self.waiting]

        following = PLAN[turn + 1] if turn + 1 < len(PLAN) else ()

        def active(args):
            outgoing, held = args
            crossed = [exchange(value, self.half) for value in outgoing]
            handed = [self.hand(value) for value in held]
            handed += [self.hand(value) for value in crossed[:direct]]
            ready = [self.cut(item) for item in following]
            return crossed, handed, *lax.optimization_barrier((ready, work()))

        def idle(_):
            empty = {}
            for name, first, units in (*items, *handing, *following):
                shape = list(self.source[name].shape)
                shape[1] = self.unit(name) * units
                empty[name, first, units] = jnp.zeros(shape, jnp.bfloat16)
            some = [[empty[item] for item in group] for group in (items, handing, following)]
            return *some, work()

        crossed, handed, self.ready, made = lax.cond(self.on, active, idle, (self.ready, held))
        self.relayed.update(zip(handing, handed))
        self.arrived.update(zip(items, crossed))
        self.waiting = items[direct:]
        return made

    def place(self, item, mine):
        name, first, units = item
        rows = self.source[name].shape[1]
        unit = self.unit(name)
        return (0 if name == "g" else 1, mine, first * unit, rows // 2, units * unit)

    def finish(self):
        likes = (self.source["g"], self.source["d"])
        held = [self.arrived[item] for item in self.waiting]
        early = [self.place(item, True) for item in self.arrived]
        early += [self.place(item, False) for item in self.relayed]
        late = [self.place(item, False) for item in self.waiting]

        def active(held):
            handed = [self.hand(value) for value in held]
            sources = list(self.arrived.values()) + list(self.relayed.values())
            begun = place_pieces(self.numbers, sources, early, likes)
            return tuple(place_pieces(self.numbers, handed, late, likes, onto=begun))

        def idle(_):
            return tuple(place_pieces(self.numbers, [], early + late, likes, True))

        return lax.cond(self.on, active, idle, held)


def staged(batches, placement, gate_up, down, swap):
    peers = lax.axis_size("expert")
    levels = peers // 4
    width = down.shape[-1]
    own = extended_rows(batches, placement)
    rows = own.shape[0]

    def ffn(first, second, joined_w):
        return weighted_ffn(first, second, peers, joined_w, down[0])

    columns = [own] + [
        lax.ppermute(own, "expert", shift_pairs(peers, 4 * hop)) for hop in range(1, levels)
    ]
    joined_w = swap.step(0, lambda: gate_up[0].reshape(width, -1))
    columns, joined_w = lax.optimization_barrier((columns, joined_w))
    here = jnp.concatenate(columns, axis=0)
    here_core = exchange(here, 1)
    across = exchange(here, 2)
    part_here, part_here_core = swap.step(1, lambda: ffn(here, here_core, joined_w))
    across, part_here_core = lax.optimization_barrier((across, part_here_core))
    across_core = exchange(across, 1)
    got_here = exchange(part_here_core, 1)
    part_across, part_across_core = swap.step(2, lambda: ffn(across, across_core, joined_w))
    got_across = exchange(part_across_core, 1)
    sum_across = (part_across + got_across.astype(jnp.float32)).astype(jnp.bfloat16)
    got_column = exchange(sum_across, 2)
    sum_here = swap.step(3, lambda: part_here + got_here.astype(jnp.float32))
    column = sum_here + got_column.astype(jnp.float32)
    total = column[:rows]
    returned = [
        lax.ppermute(
            column[hop * rows : (hop + 1) * rows].astype(jnp.bfloat16),
            "expert",
            shift_pairs(peers, peers - 4 * hop),
        )
        for hop in range(1, levels)
    ]
    new_gate_up, new_down = swap.finish()
    for value in returned:
        total = total + value.astype(jnp.float32)
    total = total.astype(jnp.bfloat16)
    return total, new_gate_up, new_down


def body(
    tokens_one,
    tokens_two,
    experts_one,
    experts_two,
    gates_one,
    gates_two,
    old_placement,
    swap_flags,
    gate_up,
    down,
):
    peer_total = lax.axis_size("expert")
    swap = Swap(swap_flags, gate_up, down)
    if lax.axis_size("tensor") == 1 and peer_total == 16:
        count = tokens_one.shape[0]
        total, new_gate_up, new_down = staged(
            ((tokens_one, experts_one, gates_one), (tokens_two, experts_two, gates_two)),
            old_placement,
            gate_up,
            down,
            swap,
        )
        return (total[:count], total[count:], new_gate_up, new_down)
    slot_index = jnp.arange(peer_total, dtype=jnp.int32)
    old_slots = slot_table(old_placement, slot_index)
    joined_w = gate_up[0].reshape(gate_up.shape[1], -1)
    outs = []
    for tokens, chosen, gates in (
        (tokens_one, experts_one, gates_one),
        (tokens_two, experts_two, gates_two),
    ):
        rows = lax.all_gather(tokens, "tensor", axis=0, tiled=True)
        outs.append(routed_layer(rows, chosen, gates, old_slots, joined_w, down[0]))
    for turn in range(len(PLAN)):
        swap.step(turn, lambda: ())
    new_gate_up, new_down = swap.finish()
    return (outs[0], outs[1], new_gate_up, new_down)


def solution(mesh):
    return jax.shard_map(
        body,
        mesh=mesh,
        in_specs=(
            P(("groups", "expert", "tensor"), None),
            P(("groups", "expert", "tensor"), None),
            P(("groups", "expert"), None),
            P(("groups", "expert"), None),
            P(("groups", "expert"), None),
            P(("groups", "expert"), None),
            P(),
            P(),
            P("expert", None, None, "tensor"),
            P("expert", "tensor", None),
        ),
        out_specs=(
            P(("groups", "expert", "tensor"), None),
            P(("groups", "expert", "tensor"), None),
            P(("groups", "expert"), None, None, "tensor"),
            P(("groups", "expert"), "tensor", None),
        ),
        check_vma=False,
    )
```

```python
import functools
import math

import jax
import jax.numpy as jnp
from jax import lax
from jax.experimental import pallas as pl
from jax.experimental.pallas import tpu as pltpu
from jax.sharding import PartitionSpec as P

LANES = 128


def xor_pairs(count, mask):
    return [(source, source ^ mask) for source in range(count)]


def shift_pairs(count, shift):
    return [(source, (source + shift) % count) for source in range(count)]


def exchange(value, mask):
    return lax.ppermute(value, "expert", xor_pairs(lax.axis_size("expert"), mask))


def slot_table(placement, slot_index):
    match_table = placement[:, None] == slot_index[None, :]
    return jnp.sum(jnp.where(match_table, slot_index[:, None], 0), axis=0)


def expert_ffn(rows, joined_w, down_w):
    half_width = down_w.shape[0]
    projected = jnp.dot(rows, joined_w, preferred_element_type=jnp.float32)
    hidden = (jax.nn.silu(projected[:, :half_width]) * projected[:, half_width:]).astype(
        jnp.bfloat16
    )
    return jnp.dot(hidden, down_w, preferred_element_type=jnp.float32)


def routed_layer(pair_rows, chosen, gates, slot_of, joined_w, down_w):
    row_total = pair_rows.shape[0]
    width = pair_rows.shape[1]
    top_count = chosen.shape[1]
    peer_total = lax.axis_size("expert")
    capacity = min(row_total, max(2, 3 * row_total * top_count // (2 * peer_total)))
    norm_gates = gates / jnp.sum(gates, axis=-1, keepdims=True)
    slot_index = jnp.arange(peer_total, dtype=jnp.int32)
    flat_ids = chosen.reshape(-1)
    expert_hot = flat_ids[:, None] == slot_index[None, :]
    target = jnp.sum(jnp.where(expert_hot, slot_of[None, :], 0), axis=1)
    target_hot = target[:, None] == slot_index[None, :]
    running = jnp.cumsum(target_hot.astype(jnp.int32), axis=0)
    position = jnp.sum(jnp.where(target_hot, running, 0), axis=1) - 1
    outgoing = jnp.zeros((peer_total, capacity, width), jnp.bfloat16)
    outgoing = outgoing.at[target, position].set(jnp.repeat(pair_rows, top_count, axis=0))
    received = lax.all_to_all(outgoing, "expert", split_axis=0, concat_axis=0, tiled=True)
    partial_rows = expert_ffn(received.reshape(-1, width), joined_w, down_w).astype(jnp.bfloat16)
    returned = lax.all_to_all(
        partial_rows.reshape(received.shape), "expert", split_axis=0, concat_axis=0, tiled=True
    )
    picked = returned[target, position].astype(jnp.float32)
    weighted = picked * norm_gates.reshape(-1)[:, None]
    partial_value = jnp.sum(weighted.reshape(row_total, top_count, width), axis=1)
    return lax.psum_scatter(partial_value, "tensor", scatter_dimension=0, tiled=True).astype(
        jnp.bfloat16
    )


def extended_kernel(placement_ref, *refs):
    out_ref = refs[-1]
    slots = placement_ref.shape[0]
    parts = (len(refs) - 1) // 3
    for number in range(parts):
        rows_ref, chosen_ref, gates_ref = refs[3 * number : 3 * number + 3]
        rows, width = rows_ref.shape
        chosen, gates = chosen_ref[...], gates_ref[...]
        weights = gates / jnp.sum(gates, axis=0, keepdims=True)
        slot = lax.broadcasted_iota(jnp.int32, (slots, rows), 0)
        dense = jnp.zeros((slots, rows), jnp.float32)
        for index in range(slots):
            named = jnp.where(chosen == placement_ref[index], weights, 0.0)
            dense = jnp.where(slot == index, jnp.sum(named, axis=0, keepdims=True), dense)
        tail = jnp.zeros((rows, LANES), jnp.float32)
        for place in range(3):
            part = dense.astype(jnp.bfloat16)
            dense = dense - part.astype(jnp.float32)
            lane = lax.broadcasted_iota(jnp.int32, (slots, LANES), 1)
            row = lax.broadcasted_iota(jnp.int32, (slots, LANES), 0)
            spot = (lane == row + place * slots).astype(jnp.float32).astype(jnp.bfloat16)
            tail += lax.dot_general(
                part, spot, (((0,), (0,)), ((), ())), preferred_element_type=jnp.float32
            )
        out_ref[number * rows : (number + 1) * rows, :width] = rows_ref[...]
        out_ref[number * rows : (number + 1) * rows, width:] = tail.astype(jnp.bfloat16)


def extended_rows(batches, placement):
    rows, width = batches[0][0].shape
    vmem = pl.BlockSpec(memory_space=pltpu.VMEM)
    given = [array for tokens, chosen, gates in batches for array in (tokens, chosen.T, gates.T)]
    return pl.pallas_call(
        extended_kernel,
        out_shape=jax.ShapeDtypeStruct((len(batches) * rows, width + LANES), jnp.bfloat16),
        in_specs=[pl.BlockSpec(memory_space=pltpu.SMEM)] + [vmem] * len(given),
        out_specs=vmem,
    )(placement, *given)


def ffn_kernel(slots, own_ref, first_ref, second_ref, gate_ref, up_ref, down_ref, near_ref, far_ref, total):
    turn, turns = pl.program_id(0), pl.num_programs(0)
    width = near_ref.shape[1]

    for number, (rows_ref, out_ref) in enumerate(((first_ref, near_ref), (second_ref, far_ref))):
        rows = rows_ref[:, :width]
        gate = jnp.dot(rows, gate_ref[...], preferred_element_type=jnp.float32)
        up = jnp.dot(rows, up_ref[...], preferred_element_type=jnp.float32)
        hidden = (jax.nn.silu(gate) * up).astype(jnp.bfloat16)
        part = jnp.dot(hidden, down_ref[...], preferred_element_type=jnp.float32)

        @pl.when(turn == 0)
        def _(number=number, part=part):
            total[number] = part

        @pl.when(turn > 0)
        def _(number=number, part=part):
            total[number] += part

        @pl.when(turn == turns - 1)
        def _(number=number, rows_ref=rows_ref, out_ref=out_ref):
            tail = rows_ref[:, width:].astype(jnp.float32)
            column = lax.broadcasted_iota(jnp.int32, tail.shape, 1)
            own = own_ref[0]
            mine = (column == own) | (column == own + slots) | (column == own + 2 * slots)
            weight = jnp.sum(jnp.where(mine, tail, 0.0), axis=1, keepdims=True)
            out_ref[...] = (weight * total[number]).astype(out_ref.dtype)


def weighted_ffn(first, second, slots, joined_w, down_w):
    rows, span = first.shape
    half_width, width = down_w.shape
    tile = 256
    tiles = half_width // tile
    own = lax.axis_index("expert").astype(jnp.int32).reshape(1)
    once = pl.Buffered(1)
    whole = pl.BlockSpec((rows, span), lambda turn: (0, 0), pipeline_mode=once)
    result = pl.BlockSpec((rows, width), lambda turn: (0, 0), pipeline_mode=once)
    return pl.pallas_call(
        functools.partial(ffn_kernel, slots),
        grid=(tiles,),
        in_specs=[
            pl.BlockSpec(memory_space=pltpu.SMEM),
            whole,
            whole,
            pl.BlockSpec((width, tile), lambda turn: (0, turn)),
            pl.BlockSpec((width, tile), lambda turn: (0, tiles + turn)),
            pl.BlockSpec((tile, width), lambda turn: (turn, 0)),
        ],
        out_specs=[result, result],
        out_shape=[
            jax.ShapeDtypeStruct((rows, width), jnp.float32),
            jax.ShapeDtypeStruct((rows, width), jnp.bfloat16),
        ],
        scratch_shapes=[pltpu.VMEM((2, rows, width), jnp.float32)],
        cost_estimate=pl.CostEstimate(
            flops=12 * rows * width * half_width,
            bytes_accessed=6 * width * half_width + 10 * rows * width,
            transcendentals=2 * rows * half_width,
        ),
        compiler_params=pltpu.CompilerParams(vmem_limit_bytes=21 << 20),
    )(own, first, second, joined_w, joined_w, down_w)


def copies_kernel(places, swaps, owns, numbers_ref, *refs):
    count = len(places)
    pieces = refs[: count if swaps else 0]
    own_refs = refs[len(pieces) : len(pieces) + 2]
    outputs, held = refs[-4 - count : -2 - count], refs[-2 - count : -2]
    in_sems, out_sems = refs[-2], refs[-1]
    group, on = numbers_ref[0], numbers_ref[1]

    def cut(refs, place):
        output, mine, first, span, rows = place
        half = group if mine else 1 - group
        start = pl.multiple_of(half * span + first, 16)
        return refs[output].at[:, pl.ds(start, rows)]

    def run(sources):
        inward = [
            pltpu.make_async_copy(source, held[k], in_sems.at[k]) for k, source in enumerate(sources)
        ]
        outward = [
            pltpu.make_async_copy(held[k], cut(outputs, place), out_sems.at[k])
            for k, place in enumerate(places)
        ]
        for copy in inward:
            copy.start()
        for arrival, departure in zip(inward, outward):
            arrival.wait()
            departure.start()
        for departure in outward:
            departure.wait()

    if swaps and owns:
        pl.when(on == 1)(lambda: run(pieces))
        pl.when(on == 0)(lambda: run([cut(own_refs, place) for place in places]))
    elif swaps:
        run(pieces)
    else:
        run([cut(own_refs, place) for place in places])


def place_pieces(numbers, sources, places, likes, owns=False, onto=None):
    anywhere = pl.BlockSpec(memory_space=pl.ANY)
    extra = list(onto) if onto is not None else []
    given = list(sources) + (list(likes) if owns else [])
    held = []
    for output, _, _, _, rows in places:
        like = likes[output]
        held.append(pltpu.VMEM((like.shape[0], rows, *like.shape[2:]), like.dtype))
    moved = sum(math.prod(one.shape) * one.dtype.itemsize for one in held)
    return pl.pallas_call(
        functools.partial(copies_kernel, places, len(sources) > 0, owns),
        out_shape=[jax.ShapeDtypeStruct(like.shape, like.dtype) for like in likes],
        in_specs=[pl.BlockSpec(memory_space=pltpu.SMEM)] + [anywhere] * (len(given) + len(extra)),
        out_specs=[anywhere] * len(likes),
        scratch_shapes=[
            *held,
            pltpu.SemaphoreType.DMA((len(held),)),
            pltpu.SemaphoreType.DMA((len(held),)),
        ],
        input_output_aliases={1 + len(given) + k: k for k in range(len(extra))},
        cost_estimate=pl.CostEstimate(flops=0, bytes_accessed=2 * moved, transcendentals=0),
        compiler_params=pltpu.CompilerParams(vmem_limit_bytes=moved + (2 << 20)),
    )(numbers, *given, *extra)


UNITS = {"g": 8, "d": 4}
PLAN = (
    (("g", 0, 2), ("g", 2, 2)),
    (("d", 0, 1), ("g", 4, 2)),
    (("d", 1, 1), ("d", 2, 1)),
    (("d", 3, 1), ("g", 6, 2)),
)
AT_ONCE = (0, 0, 0, 1)
GROUP_PAIRS = [(0, 1), (1, 0)]


class Swap:
    def __init__(self, flags, gate_up, down):
        peers = lax.axis_size("expert")
        self.peers, self.half = peers, peers // 2
        self.group = lax.axis_index("groups")
        self.source = {"g": gate_up, "d": down}
        self.on = flags[lax.axis_index("expert") % self.half] == 1
        self.numbers = jnp.stack([self.group.astype(jnp.int32), self.on.astype(jnp.int32)])
        self.arrived, self.relayed, self.waiting = {}, {}, ()
        self.ready = [self.cut(item) for item in PLAN[0]]

    def unit(self, name):
        return self.source[name].shape[1] // (2 * UNITS[name])

    def cut(self, item):
        name, first, units = item
        unit = self.unit(name)
        start = (self.group * UNITS[name] + first) * unit
        return lax.dynamic_slice_in_dim(self.source[name], start, units * unit, axis=1)

    def hand(self, value):
        return lax.ppermute(value, "groups", GROUP_PAIRS)

    def step(self, turn, work):
        items = PLAN[turn]
        direct = AT_ONCE[turn]
        handing = (*self.waiting, *items[:direct])
        held = [self.arrived[item] for item in self.waiting]

        following = PLAN[turn + 1] if turn + 1 < len(PLAN) else ()

        def active(args):
            outgoing, held = args
            crossed = [exchange(value, self.half) for value in outgoing]
            handed = [self.hand(value) for value in held]
            handed += [self.hand(value) for value in crossed[:direct]]
            ready = [self.cut(item) for item in following]
            return crossed, handed, *lax.optimization_barrier((ready, work()))

        def idle(_):
            empty = {}
            for name, first, units in (*items, *handing, *following):
                shape = list(self.source[name].shape)
                shape[1] = self.unit(name) * units
                empty[name, first, units] = jnp.zeros(shape, jnp.bfloat16)
            some = [[empty[item] for item in group] for group in (items, handing, following)]
            return *some, work()

        crossed, handed, self.ready, made = lax.cond(self.on, active, idle, (self.ready, held))
        self.relayed.update(zip(handing, handed))
        self.arrived.update(zip(items, crossed))
        self.waiting = items[direct:]
        return made

    def place(self, item, mine):
        name, first, units = item
        rows = self.source[name].shape[1]
        unit = self.unit(name)
        return (0 if name == "g" else 1, mine, first * unit, rows // 2, units * unit)

    def finish(self):
        likes = (self.source["g"], self.source["d"])
        held = [self.arrived[item] for item in self.waiting]
        early = [self.place(item, True) for item in self.arrived]
        early += [self.place(item, False) for item in self.relayed]
        late = [self.place(item, False) for item in self.waiting]

        def active(held):
            handed = [self.hand(value) for value in held]
            sources = list(self.arrived.values()) + list(self.relayed.values())
            begun = place_pieces(self.numbers, sources, early, likes)
            return tuple(place_pieces(self.numbers, handed, late, likes, onto=begun))

        def idle(_):
            return tuple(place_pieces(self.numbers, [], early + late, likes, True))

        return lax.cond(self.on, active, idle, held)


def staged(batches, placement, gate_up, down, swap):
    peers = lax.axis_size("expert")
    levels = peers // 4
    width = down.shape[-1]
    own = extended_rows(batches, placement)
    rows = own.shape[0]

    def ffn(first, second, joined_w):
        return weighted_ffn(first, second, peers, joined_w, down[0])

    columns = [own] + [
        lax.ppermute(own, "expert", shift_pairs(peers, 4 * hop)) for hop in range(1, levels)
    ]
    joined_w = swap.step(0, lambda: gate_up[0].reshape(width, -1))
    columns, joined_w = lax.optimization_barrier((columns, joined_w))
    here = jnp.concatenate(columns, axis=0)
    here_core = exchange(here, 1)
    across = exchange(here, 2)
    part_here, part_here_core = swap.step(1, lambda: ffn(here, here_core, joined_w))
    across, part_here_core = lax.optimization_barrier((across, part_here_core))
    across_core = exchange(across, 1)
    got_here = exchange(part_here_core, 1)
    part_across, part_across_core = swap.step(2, lambda: ffn(across, across_core, joined_w))
    got_across = exchange(part_across_core, 1)
    sum_across = (part_across + got_across.astype(jnp.float32)).astype(jnp.bfloat16)
    got_column = exchange(sum_across, 2)
    sum_here = swap.step(3, lambda: part_here + got_here.astype(jnp.float32))
    column = sum_here + got_column.astype(jnp.float32)
    total = column[:rows]
    returned = [
        lax.ppermute(
            column[hop * rows : (hop + 1) * rows].astype(jnp.bfloat16),
            "expert",
            shift_pairs(peers, peers - 4 * hop),
        )
        for hop in range(1, levels)
    ]
    new_gate_up, new_down = swap.finish()
    for value in returned:
        total = total + value.astype(jnp.float32)
    total = total.astype(jnp.bfloat16)
    return total, new_gate_up, new_down


def body(
    tokens_one,
    tokens_two,
    experts_one,
    experts_two,
    gates_one,
    gates_two,
    old_placement,
    swap_flags,
    gate_up,
    down,
):
    peer_total = lax.axis_size("expert")
    swap = Swap(swap_flags, gate_up, down)
    if lax.axis_size("tensor") == 1 and peer_total == 16:
        count = tokens_one.shape[0]
        total, new_gate_up, new_down = staged(
            ((tokens_one, experts_one, gates_one), (tokens_two, experts_two, gates_two)),
            old_placement,
            gate_up,
            down,
            swap,
        )
        return (total[:count], total[count:], new_gate_up, new_down)
    slot_index = jnp.arange(peer_total, dtype=jnp.int32)
    old_slots = slot_table(old_placement, slot_index)
    joined_w = gate_up[0].reshape(gate_up.shape[1], -1)
    outs = []
    for tokens, chosen, gates in (
        (tokens_one, experts_one, gates_one),
        (tokens_two, experts_two, gates_two),
    ):
        rows = lax.all_gather(tokens, "tensor", axis=0, tiled=True)
        outs.append(routed_layer(rows, chosen, gates, old_slots, joined_w, down[0]))
    for turn in range(len(PLAN)):
        swap.step(turn, lambda: ())
    new_gate_up, new_down = swap.finish()
    return (outs[0], outs[1], new_gate_up, new_down)


def solution(mesh):
    return jax.shard_map(
        body,
        mesh=mesh,
        in_specs=(
            P(("groups", "expert", "tensor"), None),
            P(("groups", "expert", "tensor"), None),
            P(("groups", "expert"), None),
            P(("groups", "expert"), None),
            P(("groups", "expert"), None),
            P(("groups", "expert"), None),
            P(),
            P(),
            P("expert", None, None, "tensor"),
            P("expert", "tensor", None),
        ),
        out_specs=(
            P(("groups", "expert", "tensor"), None),
            P(("groups", "expert", "tensor"), None),
            P(("groups", "expert"), None, None, "tensor"),
            P(("groups", "expert"), "tensor", None),
        ),
        check_vma=False,
    )
```

```python
import functools
import math

import jax
import jax.numpy as jnp
from jax import lax
from jax.experimental import pallas as pl
from jax.experimental.pallas import tpu as pltpu
from jax.sharding import PartitionSpec as P

LANES = 128


def xor_pairs(count, mask):
    return [(source, source ^ mask) for source in range(count)]


def shift_pairs(count, shift):
    return [(source, (source + shift) % count) for source in range(count)]


def exchange(value, mask):
    return lax.ppermute(value, "expert", xor_pairs(lax.axis_size("expert"), mask))


def slot_table(placement, slot_index):
    match_table = placement[:, None] == slot_index[None, :]
    return jnp.sum(jnp.where(match_table, slot_index[:, None], 0), axis=0)


def expert_ffn(rows, joined_w, down_w):
    half_width = down_w.shape[0]
    projected = jnp.dot(rows, joined_w, preferred_element_type=jnp.float32)
    hidden = (jax.nn.silu(projected[:, :half_width]) * projected[:, half_width:]).astype(
        jnp.bfloat16
    )
    return jnp.dot(hidden, down_w, preferred_element_type=jnp.float32)


def routed_layer(pair_rows, chosen, gates, slot_of, joined_w, down_w):
    row_total = pair_rows.shape[0]
    width = pair_rows.shape[1]
    top_count = chosen.shape[1]
    peer_total = lax.axis_size("expert")
    capacity = min(row_total, max(2, 3 * row_total * top_count // (2 * peer_total)))
    norm_gates = gates / jnp.sum(gates, axis=-1, keepdims=True)
    slot_index = jnp.arange(peer_total, dtype=jnp.int32)
    flat_ids = chosen.reshape(-1)
    expert_hot = flat_ids[:, None] == slot_index[None, :]
    target = jnp.sum(jnp.where(expert_hot, slot_of[None, :], 0), axis=1)
    target_hot = target[:, None] == slot_index[None, :]
    running = jnp.cumsum(target_hot.astype(jnp.int32), axis=0)
    position = jnp.sum(jnp.where(target_hot, running, 0), axis=1) - 1
    outgoing = jnp.zeros((peer_total, capacity, width), jnp.bfloat16)
    outgoing = outgoing.at[target, position].set(jnp.repeat(pair_rows, top_count, axis=0))
    received = lax.all_to_all(outgoing, "expert", split_axis=0, concat_axis=0, tiled=True)
    partial_rows = expert_ffn(received.reshape(-1, width), joined_w, down_w).astype(jnp.bfloat16)
    returned = lax.all_to_all(
        partial_rows.reshape(received.shape), "expert", split_axis=0, concat_axis=0, tiled=True
    )
    picked = returned[target, position].astype(jnp.float32)
    weighted = picked * norm_gates.reshape(-1)[:, None]
    partial_value = jnp.sum(weighted.reshape(row_total, top_count, width), axis=1)
    return lax.psum_scatter(partial_value, "tensor", scatter_dimension=0, tiled=True).astype(
        jnp.bfloat16
    )


def extended_kernel(placement_ref, *refs):
    out_ref = refs[-1]
    slots = placement_ref.shape[0]
    parts = (len(refs) - 1) // 3
    for number in range(parts):
        rows_ref, chosen_ref, gates_ref = refs[3 * number : 3 * number + 3]
        rows, width = rows_ref.shape
        chosen, gates = chosen_ref[...], gates_ref[...]
        weights = gates / jnp.sum(gates, axis=0, keepdims=True)
        slot = lax.broadcasted_iota(jnp.int32, (slots, rows), 0)
        dense = jnp.zeros((slots, rows), jnp.float32)
        for index in range(slots):
            named = jnp.where(chosen == placement_ref[index], weights, 0.0)
            dense = jnp.where(slot == index, jnp.sum(named, axis=0, keepdims=True), dense)
        tail = jnp.zeros((rows, LANES), jnp.float32)
        for place in range(3):
            part = dense.astype(jnp.bfloat16)
            dense = dense - part.astype(jnp.float32)
            lane = lax.broadcasted_iota(jnp.int32, (slots, LANES), 1)
            row = lax.broadcasted_iota(jnp.int32, (slots, LANES), 0)
            spot = (lane == row + place * slots).astype(jnp.float32).astype(jnp.bfloat16)
            tail += lax.dot_general(
                part, spot, (((0,), (0,)), ((), ())), preferred_element_type=jnp.float32
            )
        out_ref[number * rows : (number + 1) * rows, :width] = rows_ref[...]
        out_ref[number * rows : (number + 1) * rows, width:] = tail.astype(jnp.bfloat16)


def extended_rows(batches, placement):
    rows, width = batches[0][0].shape
    vmem = pl.BlockSpec(memory_space=pltpu.VMEM)
    given = [array for tokens, chosen, gates in batches for array in (tokens, chosen.T, gates.T)]
    return pl.pallas_call(
        extended_kernel,
        out_shape=jax.ShapeDtypeStruct((len(batches) * rows, width + LANES), jnp.bfloat16),
        in_specs=[pl.BlockSpec(memory_space=pltpu.SMEM)] + [vmem] * len(given),
        out_specs=vmem,
    )(placement, *given)


def joined_rows(pieces):
    def kernel(*refs):
        start = 0
        for ref in refs[:-1]:
            refs[-1][start : start + ref.shape[0]] = ref[...]
            start += ref.shape[0]

    vmem = pl.BlockSpec(memory_space=pltpu.VMEM)
    total = sum(piece.shape[0] for piece in pieces)
    return pl.pallas_call(
        kernel,
        out_shape=jax.ShapeDtypeStruct((total, pieces[0].shape[1]), pieces[0].dtype),
        in_specs=[vmem] * len(pieces),
        out_specs=vmem,
    )(*pieces)


def ffn_kernel(slots, own_ref, first_ref, second_ref, gate_ref, up_ref, down_ref, near_ref, far_ref, total):
    turn, turns = pl.program_id(0), pl.num_programs(0)
    width = near_ref.shape[1]

    for number, (rows_ref, out_ref) in enumerate(((first_ref, near_ref), (second_ref, far_ref))):
        rows = rows_ref[:, :width]
        gate = jnp.dot(rows, gate_ref[...], preferred_element_type=jnp.float32)
        up = jnp.dot(rows, up_ref[...], preferred_element_type=jnp.float32)
        hidden = (jax.nn.silu(gate) * up).astype(jnp.bfloat16)
        part = jnp.dot(hidden, down_ref[...], preferred_element_type=jnp.float32)

        @pl.when(turn == 0)
        def _(number=number, part=part):
            total[number] = part

        @pl.when(turn > 0)
        def _(number=number, part=part):
            total[number] += part

        @pl.when(turn == turns - 1)
        def _(number=number, rows_ref=rows_ref, out_ref=out_ref):
            tail = rows_ref[:, width:].astype(jnp.float32)
            column = lax.broadcasted_iota(jnp.int32, tail.shape, 1)
            own = own_ref[0]
            mine = (column == own) | (column == own + slots) | (column == own + 2 * slots)
            weight = jnp.sum(jnp.where(mine, tail, 0.0), axis=1, keepdims=True)
            out_ref[...] = (weight * total[number]).astype(out_ref.dtype)


def weighted_ffn(first, second, slots, joined_w, down_w):
    rows, span = first.shape
    half_width, width = down_w.shape
    tile = 256
    tiles = half_width // tile
    own = lax.axis_index("expert").astype(jnp.int32).reshape(1)
    once = pl.Buffered(1)
    whole = pl.BlockSpec((rows, span), lambda turn: (0, 0), pipeline_mode=once)
    result = pl.BlockSpec((rows, width), lambda turn: (0, 0), pipeline_mode=once)
    return pl.pallas_call(
        functools.partial(ffn_kernel, slots),
        grid=(tiles,),
        in_specs=[
            pl.BlockSpec(memory_space=pltpu.SMEM),
            whole,
            whole,
            pl.BlockSpec((width, tile), lambda turn: (0, turn)),
            pl.BlockSpec((width, tile), lambda turn: (0, tiles + turn)),
            pl.BlockSpec((tile, width), lambda turn: (turn, 0)),
        ],
        out_specs=[result, result],
        out_shape=[
            jax.ShapeDtypeStruct((rows, width), jnp.float32),
            jax.ShapeDtypeStruct((rows, width), jnp.bfloat16),
        ],
        scratch_shapes=[pltpu.VMEM((2, rows, width), jnp.float32)],
        cost_estimate=pl.CostEstimate(
            flops=12 * rows * width * half_width,
            bytes_accessed=6 * width * half_width + 10 * rows * width,
            transcendentals=2 * rows * half_width,
        ),
        compiler_params=pltpu.CompilerParams(vmem_limit_bytes=21 << 20),
    )(own, first, second, joined_w, joined_w, down_w)


def copies_kernel(places, swaps, owns, numbers_ref, *refs):
    count = len(places)
    pieces = refs[: count if swaps else 0]
    own_refs = refs[len(pieces) : len(pieces) + 2]
    outputs, held = refs[-4 - count : -2 - count], refs[-2 - count : -2]
    in_sems, out_sems = refs[-2], refs[-1]
    group, on = numbers_ref[0], numbers_ref[1]

    def cut(refs, place):
        output, mine, first, span, rows = place
        half = group if mine else 1 - group
        start = pl.multiple_of(half * span + first, 16)
        return refs[output].at[:, pl.ds(start, rows)]

    def run(sources):
        inward = [
            pltpu.make_async_copy(source, held[k], in_sems.at[k]) for k, source in enumerate(sources)
        ]
        outward = [
            pltpu.make_async_copy(held[k], cut(outputs, place), out_sems.at[k])
            for k, place in enumerate(places)
        ]
        for copy in inward:
            copy.start()
        for arrival, departure in zip(inward, outward):
            arrival.wait()
            departure.start()
        for departure in outward:
            departure.wait()

    if swaps and owns:
        pl.when(on == 1)(lambda: run(pieces))
        pl.when(on == 0)(lambda: run([cut(own_refs, place) for place in places]))
    elif swaps:
        run(pieces)
    else:
        run([cut(own_refs, place) for place in places])


def place_pieces(numbers, sources, places, likes, owns=False, onto=None):
    anywhere = pl.BlockSpec(memory_space=pl.ANY)
    extra = list(onto) if onto is not None else []
    given = list(sources) + (list(likes) if owns else [])
    held = []
    for output, _, _, _, rows in places:
        like = likes[output]
        held.append(pltpu.VMEM((like.shape[0], rows, *like.shape[2:]), like.dtype))
    moved = sum(math.prod(one.shape) * one.dtype.itemsize for one in held)
    return pl.pallas_call(
        functools.partial(copies_kernel, places, len(sources) > 0, owns),
        out_shape=[jax.ShapeDtypeStruct(like.shape, like.dtype) for like in likes],
        in_specs=[pl.BlockSpec(memory_space=pltpu.SMEM)] + [anywhere] * (len(given) + len(extra)),
        out_specs=[anywhere] * len(likes),
        scratch_shapes=[
            *held,
            pltpu.SemaphoreType.DMA((len(held),)),
            pltpu.SemaphoreType.DMA((len(held),)),
        ],
        input_output_aliases={1 + len(given) + k: k for k in range(len(extra))},
        cost_estimate=pl.CostEstimate(flops=0, bytes_accessed=2 * moved, transcendentals=0),
        compiler_params=pltpu.CompilerParams(vmem_limit_bytes=moved + (2 << 20)),
    )(numbers, *given, *extra)


UNITS = {"g": 8, "d": 4}
PLAN = (
    (("g", 0, 2),),
    (("d", 0, 1),),
    (("d", 1, 1), ("g", 2, 2)),
    (("d", 2, 1), ("d", 3, 1)),
    (("g", 4, 1), ("g", 5, 2)),
    (("g", 7, 1),),
)
AT_ONCE = (0, 0, 0, 0, 1, 0)
GROUP_PAIRS = [(0, 1), (1, 0)]


class Swap:
    def __init__(self, flags, gate_up, down):
        peers = lax.axis_size("expert")
        self.peers, self.half = peers, peers // 2
        self.group = lax.axis_index("groups")
        self.source = {"g": gate_up, "d": down}
        self.on = flags[lax.axis_index("expert") % self.half] == 1
        self.numbers = jnp.stack([self.group.astype(jnp.int32), self.on.astype(jnp.int32)])
        self.arrived, self.relayed, self.waiting = {}, {}, ()
        self.ready = [self.cut(item) for item in PLAN[0]]

    def unit(self, name):
        return self.source[name].shape[1] // (2 * UNITS[name])

    def cut(self, item):
        name, first, units = item
        unit = self.unit(name)
        start = (self.group * UNITS[name] + first) * unit
        return lax.dynamic_slice_in_dim(self.source[name], start, units * unit, axis=1)

    def hand(self, value):
        return lax.ppermute(value, "groups", GROUP_PAIRS)

    def step(self, turn, work):
        items = PLAN[turn]
        direct = AT_ONCE[turn]
        handing = (*self.waiting, *items[:direct])
        held = [self.arrived[item] for item in self.waiting]

        following = PLAN[turn + 1] if turn + 1 < len(PLAN) else ()

        def active(args):
            outgoing, held = args
            crossed = [exchange(value, self.half) for value in outgoing]
            handed = [self.hand(value) for value in held]
            handed += [self.hand(value) for value in crossed[:direct]]
            ready = [self.cut(item) for item in following]
            return crossed, handed, *lax.optimization_barrier((ready, work()))

        def idle(_):
            empty = {}
            for name, first, units in (*items, *handing, *following):
                shape = list(self.source[name].shape)
                shape[1] = self.unit(name) * units
                empty[name, first, units] = jnp.zeros(shape, jnp.bfloat16)
            some = [[empty[item] for item in group] for group in (items, handing, following)]
            return *some, work()

        crossed, handed, self.ready, made = lax.cond(self.on, active, idle, (self.ready, held))
        self.relayed.update(zip(handing, handed))
        self.arrived.update(zip(items, crossed))
        self.waiting = items[direct:]
        return made

    def place(self, item, mine):
        name, first, units = item
        rows = self.source[name].shape[1]
        unit = self.unit(name)
        return (0 if name == "g" else 1, mine, first * unit, rows // 2, units * unit)

    def finish(self):
        likes = (self.source["g"], self.source["d"])
        held = [self.arrived[item] for item in self.waiting]
        early = [self.place(item, True) for item in self.arrived]
        early += [self.place(item, False) for item in self.relayed]
        late = [self.place(item, False) for item in self.waiting]

        def active(held):
            handed = [self.hand(value) for value in held]
            sources = list(self.arrived.values()) + list(self.relayed.values())
            begun = place_pieces(self.numbers, sources, early, likes)
            return tuple(place_pieces(self.numbers, handed, late, likes, onto=begun))

        def idle(_):
            return tuple(place_pieces(self.numbers, [], early + late, likes, True))

        return lax.cond(self.on, active, idle, held)


def staged(batches, placement, gate_up, down, swap):
    peers = lax.axis_size("expert")
    width = down.shape[-1]
    own = extended_rows(batches, placement)
    rows = own.shape[0]

    def ffn(first, second, joined_w):
        return weighted_ffn(first, second, peers, joined_w, down[0])

    opposite = exchange(own, 8)
    kept = swap.step(0, lambda: own + 0)
    opposite, kept = lax.optimization_barrier((opposite, kept))
    pair = joined_rows((kept, opposite))
    beside = exchange(pair, 4)
    joined_w = swap.step(1, lambda: gate_up[0].reshape(width, -1))
    beside, joined_w = lax.optimization_barrier((beside, joined_w))
    here = joined_rows((pair, beside))
    here_core = exchange(here, 1)
    across = exchange(here, 2)
    part_here, part_here_core = swap.step(2, lambda: ffn(here, here_core, joined_w))
    across, part_here_core = lax.optimization_barrier((across, part_here_core))
    across_core = exchange(across, 1)
    got_here = exchange(part_here_core, 1)
    part_across, part_across_core = swap.step(3, lambda: ffn(across, across_core, joined_w))
    got_across = exchange(part_across_core, 1)
    sum_across = (part_across + got_across.astype(jnp.float32)).astype(jnp.bfloat16)
    got_column = exchange(sum_across, 2)
    sum_here = swap.step(4, lambda: part_here + got_here.astype(jnp.float32))
    sent = sum_here[2 * rows :] + got_column[2 * rows :].astype(jnp.float32)
    got_beside = exchange(sent.astype(jnp.bfloat16), 4)
    mine = swap.step(
        5, lambda: sum_here[: 2 * rows] + got_column[: 2 * rows].astype(jnp.float32)
    )
    mine = mine + got_beside.astype(jnp.float32)
    returned = exchange(mine[rows:].astype(jnp.bfloat16), 8)
    new_gate_up, new_down = swap.finish()
    total = (mine[:rows] + returned.astype(jnp.float32)).astype(jnp.bfloat16)
    return total, new_gate_up, new_down


def body(
    tokens_one,
    tokens_two,
    experts_one,
    experts_two,
    gates_one,
    gates_two,
    old_placement,
    swap_flags,
    gate_up,
    down,
):
    peer_total = lax.axis_size("expert")
    swap = Swap(swap_flags, gate_up, down)
    if lax.axis_size("tensor") == 1 and peer_total == 16:
        count = tokens_one.shape[0]
        total, new_gate_up, new_down = staged(
            ((tokens_one, experts_one, gates_one), (tokens_two, experts_two, gates_two)),
            old_placement,
            gate_up,
            down,
            swap,
        )
        return (total[:count], total[count:], new_gate_up, new_down)
    slot_index = jnp.arange(peer_total, dtype=jnp.int32)
    old_slots = slot_table(old_placement, slot_index)
    joined_w = gate_up[0].reshape(gate_up.shape[1], -1)
    outs = []
    for tokens, chosen, gates in (
        (tokens_one, experts_one, gates_one),
        (tokens_two, experts_two, gates_two),
    ):
        rows = lax.all_gather(tokens, "tensor", axis=0, tiled=True)
        outs.append(routed_layer(rows, chosen, gates, old_slots, joined_w, down[0]))
    for turn in range(len(PLAN)):
        swap.step(turn, lambda: ())
    new_gate_up, new_down = swap.finish()
    return (outs[0], outs[1], new_gate_up, new_down)


def solution(mesh):
    return jax.shard_map(
        body,
        mesh=mesh,
        in_specs=(
            P(("groups", "expert", "tensor"), None),
            P(("groups", "expert", "tensor"), None),
            P(("groups", "expert"), None),
            P(("groups", "expert"), None),
            P(("groups", "expert"), None),
            P(("groups", "expert"), None),
            P(),
            P(),
            P("expert", None, None, "tensor"),
            P("expert", "tensor", None),
        ),
        out_specs=(
            P(("groups", "expert", "tensor"), None),
            P(("groups", "expert", "tensor"), None),
            P(("groups", "expert"), None, None, "tensor"),
            P(("groups", "expert"), "tensor", None),
        ),
        check_vma=False,
    )
```

```python
import functools
import math

import jax
import jax.numpy as jnp
from jax import lax
from jax.experimental import pallas as pl
from jax.experimental.pallas import tpu as pltpu
from jax.sharding import PartitionSpec as P

LANES = 128


def xor_pairs(count, mask):
    return [(source, source ^ mask) for source in range(count)]


def shift_pairs(count, shift):
    return [(source, (source + shift) % count) for source in range(count)]


def exchange(value, mask):
    return lax.ppermute(value, "expert", xor_pairs(lax.axis_size("expert"), mask))


def slot_table(placement, slot_index):
    match_table = placement[:, None] == slot_index[None, :]
    return jnp.sum(jnp.where(match_table, slot_index[:, None], 0), axis=0)


def expert_ffn(rows, joined_w, down_w):
    half_width = down_w.shape[0]
    projected = jnp.dot(rows, joined_w, preferred_element_type=jnp.float32)
    hidden = (jax.nn.silu(projected[:, :half_width]) * projected[:, half_width:]).astype(
        jnp.bfloat16
    )
    return jnp.dot(hidden, down_w, preferred_element_type=jnp.float32)


def routed_layer(pair_rows, chosen, gates, slot_of, joined_w, down_w):
    row_total = pair_rows.shape[0]
    width = pair_rows.shape[1]
    top_count = chosen.shape[1]
    peer_total = lax.axis_size("expert")
    capacity = min(row_total, max(2, 3 * row_total * top_count // (2 * peer_total)))
    norm_gates = gates / jnp.sum(gates, axis=-1, keepdims=True)
    slot_index = jnp.arange(peer_total, dtype=jnp.int32)
    flat_ids = chosen.reshape(-1)
    expert_hot = flat_ids[:, None] == slot_index[None, :]
    target = jnp.sum(jnp.where(expert_hot, slot_of[None, :], 0), axis=1)
    target_hot = target[:, None] == slot_index[None, :]
    running = jnp.cumsum(target_hot.astype(jnp.int32), axis=0)
    position = jnp.sum(jnp.where(target_hot, running, 0), axis=1) - 1
    outgoing = jnp.zeros((peer_total, capacity, width), jnp.bfloat16)
    outgoing = outgoing.at[target, position].set(jnp.repeat(pair_rows, top_count, axis=0))
    received = lax.all_to_all(outgoing, "expert", split_axis=0, concat_axis=0, tiled=True)
    partial_rows = expert_ffn(received.reshape(-1, width), joined_w, down_w).astype(jnp.bfloat16)
    returned = lax.all_to_all(
        partial_rows.reshape(received.shape), "expert", split_axis=0, concat_axis=0, tiled=True
    )
    picked = returned[target, position].astype(jnp.float32)
    weighted = picked * norm_gates.reshape(-1)[:, None]
    partial_value = jnp.sum(weighted.reshape(row_total, top_count, width), axis=1)
    return lax.psum_scatter(partial_value, "tensor", scatter_dimension=0, tiled=True).astype(
        jnp.bfloat16
    )


def extended_kernel(placement_ref, *refs):
    out_ref = refs[-1]
    slots = placement_ref.shape[0]
    parts = (len(refs) - 1) // 3
    for number in range(parts):
        rows_ref, chosen_ref, gates_ref = refs[3 * number : 3 * number + 3]
        rows, width = rows_ref.shape
        chosen, gates = chosen_ref[...], gates_ref[...]
        weights = gates / jnp.sum(gates, axis=0, keepdims=True)
        slot = lax.broadcasted_iota(jnp.int32, (slots, rows), 0)
        dense = jnp.zeros((slots, rows), jnp.float32)
        for index in range(slots):
            named = jnp.where(chosen == placement_ref[index], weights, 0.0)
            dense = jnp.where(slot == index, jnp.sum(named, axis=0, keepdims=True), dense)
        tail = jnp.zeros((rows, LANES), jnp.float32)
        for place in range(3):
            part = dense.astype(jnp.bfloat16)
            dense = dense - part.astype(jnp.float32)
            lane = lax.broadcasted_iota(jnp.int32, (slots, LANES), 1)
            row = lax.broadcasted_iota(jnp.int32, (slots, LANES), 0)
            spot = (lane == row + place * slots).astype(jnp.float32).astype(jnp.bfloat16)
            tail += lax.dot_general(
                part, spot, (((0,), (0,)), ((), ())), preferred_element_type=jnp.float32
            )
        out_ref[number * rows : (number + 1) * rows, :width] = rows_ref[...]
        out_ref[number * rows : (number + 1) * rows, width:] = tail.astype(jnp.bfloat16)


def extended_rows(batches, placement):
    rows, width = batches[0][0].shape
    vmem = pl.BlockSpec(memory_space=pltpu.VMEM)
    given = [array for tokens, chosen, gates in batches for array in (tokens, chosen.T, gates.T)]
    return pl.pallas_call(
        extended_kernel,
        out_shape=jax.ShapeDtypeStruct((len(batches) * rows, width + LANES), jnp.bfloat16),
        in_specs=[pl.BlockSpec(memory_space=pltpu.SMEM)] + [vmem] * len(given),
        out_specs=vmem,
    )(placement, *given)


def joined_rows(pieces):
    def kernel(*refs):
        start = 0
        for ref in refs[:-1]:
            refs[-1][start : start + ref.shape[0]] = ref[...]
            start += ref.shape[0]

    vmem = pl.BlockSpec(memory_space=pltpu.VMEM)
    total = sum(piece.shape[0] for piece in pieces)
    return pl.pallas_call(
        kernel,
        out_shape=jax.ShapeDtypeStruct((total, pieces[0].shape[1]), pieces[0].dtype),
        in_specs=[vmem] * len(pieces),
        out_specs=vmem,
    )(*pieces)


def ffn_kernel(
    slots, own_ref, first_ref, second_ref, gate_ref, up_ref, down_ref, near_ref, far_ref, total, stacked
):
    turn, turns = pl.program_id(0), pl.num_programs(0)
    count, width = near_ref.shape

    @pl.when(turn == 0)
    def _():
        stacked[:count] = first_ref[:, :width]
        stacked[count:] = second_ref[:, :width]

    rows = stacked[...]
    gate = jnp.dot(rows, gate_ref[...], preferred_element_type=jnp.float32)
    up = jnp.dot(rows, up_ref[...], preferred_element_type=jnp.float32)
    hidden = (jax.nn.silu(gate) * up).astype(jnp.bfloat16)
    part = jnp.dot(hidden, down_ref[...], preferred_element_type=jnp.float32)

    @pl.when(turn == 0)
    def _():
        total[...] = part

    @pl.when((turn > 0) & (turn < turns - 1))
    def _():
        total[...] += part

    @pl.when(turn == turns - 1)
    def _():
        for number, (rows_ref, out_ref) in enumerate(((first_ref, near_ref), (second_ref, far_ref))):
            tail = rows_ref[:, width:].astype(jnp.float32)
            column = lax.broadcasted_iota(jnp.int32, tail.shape, 1)
            own = own_ref[0]
            mine = (column == own) | (column == own + slots) | (column == own + 2 * slots)
            weight = jnp.sum(jnp.where(mine, tail, 0.0), axis=1, keepdims=True)
            span = slice(number * count, (number + 1) * count)
            out_ref[...] = (weight * (total[span] + part[span])).astype(out_ref.dtype)


def weighted_ffn(first, second, slots, joined_w, down_w):
    rows, span = first.shape
    half_width, width = down_w.shape
    tile = 256
    tiles = half_width // tile
    own = lax.axis_index("expert").astype(jnp.int32).reshape(1)
    once = pl.Buffered(1)
    whole = pl.BlockSpec((rows, span), lambda turn: (0, 0), pipeline_mode=once)
    result = pl.BlockSpec((rows, width), lambda turn: (0, 0), pipeline_mode=once)
    return pl.pallas_call(
        functools.partial(ffn_kernel, slots),
        grid=(tiles,),
        in_specs=[
            pl.BlockSpec(memory_space=pltpu.SMEM),
            whole,
            whole,
            pl.BlockSpec((width, tile), lambda turn: (0, turn)),
            pl.BlockSpec((width, tile), lambda turn: (0, tiles + turn)),
            pl.BlockSpec((tile, width), lambda turn: (turn, 0)),
        ],
        out_specs=[result, result],
        out_shape=[
            jax.ShapeDtypeStruct((rows, width), jnp.float32),
            jax.ShapeDtypeStruct((rows, width), jnp.bfloat16),
        ],
        scratch_shapes=[
            pltpu.VMEM((2 * rows, width), jnp.float32),
            pltpu.VMEM((2 * rows, width), jnp.bfloat16),
        ],
        cost_estimate=pl.CostEstimate(
            flops=12 * rows * width * half_width,
            bytes_accessed=6 * width * half_width + 10 * rows * width,
            transcendentals=2 * rows * half_width,
        ),
        compiler_params=pltpu.CompilerParams(vmem_limit_bytes=28 << 20),
    )(own, first, second, joined_w, joined_w, down_w)


def copies_kernel(places, swaps, owns, numbers_ref, *refs):
    count = len(places)
    pieces = refs[: count if swaps else 0]
    own_refs = refs[len(pieces) : len(pieces) + 2]
    outputs, held = refs[-4 - count : -2 - count], refs[-2 - count : -2]
    in_sems, out_sems = refs[-2], refs[-1]
    group, on = numbers_ref[0], numbers_ref[1]

    def cut(refs, place):
        output, mine, first, span, rows = place
        half = group if mine else 1 - group
        start = pl.multiple_of(half * span + first, 16)
        return refs[output].at[:, pl.ds(start, rows)]

    def run(sources):
        inward = [
            pltpu.make_async_copy(source, held[k], in_sems.at[k]) for k, source in enumerate(sources)
        ]
        outward = [
            pltpu.make_async_copy(held[k], cut(outputs, place), out_sems.at[k])
            for k, place in enumerate(places)
        ]
        for copy in inward:
            copy.start()
        for arrival, departure in zip(inward, outward):
            arrival.wait()
            departure.start()
        for departure in outward:
            departure.wait()

    if swaps and owns:
        pl.when(on == 1)(lambda: run(pieces))
        pl.when(on == 0)(lambda: run([cut(own_refs, place) for place in places]))
    elif swaps:
        run(pieces)
    else:
        run([cut(own_refs, place) for place in places])


def place_pieces(numbers, sources, places, likes, owns=False, onto=None):
    anywhere = pl.BlockSpec(memory_space=pl.ANY)
    extra = list(onto) if onto is not None else []
    given = list(sources) + (list(likes) if owns else [])
    held = []
    for output, _, _, _, rows in places:
        like = likes[output]
        held.append(pltpu.VMEM((like.shape[0], rows, *like.shape[2:]), like.dtype))
    moved = sum(math.prod(one.shape) * one.dtype.itemsize for one in held)
    return pl.pallas_call(
        functools.partial(copies_kernel, places, len(sources) > 0, owns),
        out_shape=[jax.ShapeDtypeStruct(like.shape, like.dtype) for like in likes],
        in_specs=[pl.BlockSpec(memory_space=pltpu.SMEM)] + [anywhere] * (len(given) + len(extra)),
        out_specs=[anywhere] * len(likes),
        scratch_shapes=[
            *held,
            pltpu.SemaphoreType.DMA((len(held),)),
            pltpu.SemaphoreType.DMA((len(held),)),
        ],
        input_output_aliases={1 + len(given) + k: k for k in range(len(extra))},
        cost_estimate=pl.CostEstimate(flops=0, bytes_accessed=2 * moved, transcendentals=0),
        compiler_params=pltpu.CompilerParams(vmem_limit_bytes=moved + (2 << 20)),
    )(numbers, *given, *extra)


UNITS = {"g": 8, "d": 4}
PLAN = (
    (("g", 0, 2),),
    (("d", 0, 1),),
    (("d", 1, 1), ("g", 2, 2)),
    (("d", 2, 1), ("d", 3, 1)),
    (("g", 4, 1), ("g", 5, 2)),
    (("g", 7, 1),),
)
AT_ONCE = (0, 0, 0, 0, 1, 0)
GROUP_PAIRS = [(0, 1), (1, 0)]


class Swap:
    def __init__(self, flags, gate_up, down):
        peers = lax.axis_size("expert")
        self.peers, self.half = peers, peers // 2
        self.group = lax.axis_index("groups")
        self.source = {"g": gate_up, "d": down}
        self.on = flags[lax.axis_index("expert") % self.half] == 1
        self.numbers = jnp.stack([self.group.astype(jnp.int32), self.on.astype(jnp.int32)])
        self.arrived, self.relayed, self.waiting = {}, {}, ()
        self.ready = [self.cut(item) for item in PLAN[0]]

    def unit(self, name):
        return self.source[name].shape[1] // (2 * UNITS[name])

    def cut(self, item):
        name, first, units = item
        unit = self.unit(name)
        start = (self.group * UNITS[name] + first) * unit
        return lax.dynamic_slice_in_dim(self.source[name], start, units * unit, axis=1)

    def hand(self, value):
        return lax.ppermute(value, "groups", GROUP_PAIRS)

    def step(self, turn, work):
        items = PLAN[turn]
        direct = AT_ONCE[turn]
        handing = (*self.waiting, *items[:direct])
        held = [self.arrived[item] for item in self.waiting]

        following = PLAN[turn + 1] if turn + 1 < len(PLAN) else ()

        def active(args):
            outgoing, held = args
            crossed = [exchange(value, self.half) for value in outgoing]
            handed = [self.hand(value) for value in held]
            handed += [self.hand(value) for value in crossed[:direct]]
            ready = [self.cut(item) for item in following]
            return crossed, handed, *lax.optimization_barrier((ready, work()))

        def idle(_):
            empty = {}
            for name, first, units in (*items, *handing, *following):
                shape = list(self.source[name].shape)
                shape[1] = self.unit(name) * units
                empty[name, first, units] = jnp.zeros(shape, jnp.bfloat16)
            some = [[empty[item] for item in group] for group in (items, handing, following)]
            return *some, work()

        crossed, handed, self.ready, made = lax.cond(self.on, active, idle, (self.ready, held))
        self.relayed.update(zip(handing, handed))
        self.arrived.update(zip(items, crossed))
        self.waiting = items[direct:]
        return made

    def place(self, item, mine):
        name, first, units = item
        rows = self.source[name].shape[1]
        unit = self.unit(name)
        return (0 if name == "g" else 1, mine, first * unit, rows // 2, units * unit)

    def finish(self):
        likes = (self.source["g"], self.source["d"])
        held = [self.arrived[item] for item in self.waiting]
        early = [self.place(item, True) for item in self.arrived]
        early += [self.place(item, False) for item in self.relayed]
        late = [self.place(item, False) for item in self.waiting]

        def active(held):
            handed = [self.hand(value) for value in held]
            sources = list(self.arrived.values()) + list(self.relayed.values())
            begun = place_pieces(self.numbers, sources, early, likes)
            return tuple(place_pieces(self.numbers, handed, late, likes, onto=begun))

        def idle(_):
            return tuple(place_pieces(self.numbers, [], early + late, likes, True))

        return lax.cond(self.on, active, idle, held)


def staged(batches, placement, gate_up, down, swap):
    peers = lax.axis_size("expert")
    width = down.shape[-1]
    own = extended_rows(batches, placement)
    rows = own.shape[0]

    def ffn(first, second, joined_w):
        return weighted_ffn(first, second, peers, joined_w, down[0])

    opposite = exchange(own, 8)
    kept = swap.step(0, lambda: own + 0)
    opposite, kept = lax.optimization_barrier((opposite, kept))
    pair = joined_rows((kept, opposite))
    beside = exchange(pair, 4)
    joined_w = swap.step(1, lambda: gate_up[0].reshape(width, -1))
    beside, joined_w = lax.optimization_barrier((beside, joined_w))
    here = joined_rows((pair, beside))
    here_core = exchange(here, 1)
    across = exchange(here, 2)
    part_here, part_here_core = swap.step(2, lambda: ffn(here, here_core, joined_w))
    across, part_here_core = lax.optimization_barrier((across, part_here_core))
    across_core = exchange(across, 1)
    got_here = exchange(part_here_core, 1)
    part_across, part_across_core = swap.step(3, lambda: ffn(across, across_core, joined_w))
    got_across = exchange(part_across_core, 1)
    sum_across = (part_across + got_across.astype(jnp.float32)).astype(jnp.bfloat16)
    got_column = exchange(sum_across, 2)
    sum_here = swap.step(4, lambda: part_here + got_here.astype(jnp.float32))
    sent = sum_here[2 * rows :] + got_column[2 * rows :].astype(jnp.float32)
    got_beside = exchange(sent.astype(jnp.bfloat16), 4)
    mine = swap.step(
        5, lambda: sum_here[: 2 * rows] + got_column[: 2 * rows].astype(jnp.float32)
    )
    mine = mine + got_beside.astype(jnp.float32)
    returned = exchange(mine[rows:].astype(jnp.bfloat16), 8)
    new_gate_up, new_down = swap.finish()
    total = (mine[:rows] + returned.astype(jnp.float32)).astype(jnp.bfloat16)
    return total, new_gate_up, new_down


def body(
    tokens_one,
    tokens_two,
    experts_one,
    experts_two,
    gates_one,
    gates_two,
    old_placement,
    swap_flags,
    gate_up,
    down,
):
    peer_total = lax.axis_size("expert")
    swap = Swap(swap_flags, gate_up, down)
    if lax.axis_size("tensor") == 1 and peer_total == 16:
        count = tokens_one.shape[0]
        total, new_gate_up, new_down = staged(
            ((tokens_one, experts_one, gates_one), (tokens_two, experts_two, gates_two)),
            old_placement,
            gate_up,
            down,
            swap,
        )
        return (total[:count], total[count:], new_gate_up, new_down)
    slot_index = jnp.arange(peer_total, dtype=jnp.int32)
    old_slots = slot_table(old_placement, slot_index)
    joined_w = gate_up[0].reshape(gate_up.shape[1], -1)
    outs = []
    for tokens, chosen, gates in (
        (tokens_one, experts_one, gates_one),
        (tokens_two, experts_two, gates_two),
    ):
        rows = lax.all_gather(tokens, "tensor", axis=0, tiled=True)
        outs.append(routed_layer(rows, chosen, gates, old_slots, joined_w, down[0]))
    for turn in range(len(PLAN)):
        swap.step(turn, lambda: ())
    new_gate_up, new_down = swap.finish()
    return (outs[0], outs[1], new_gate_up, new_down)


def solution(mesh):
    return jax.shard_map(
        body,
        mesh=mesh,
        in_specs=(
            P(("groups", "expert", "tensor"), None),
            P(("groups", "expert", "tensor"), None),
            P(("groups", "expert"), None),
            P(("groups", "expert"), None),
            P(("groups", "expert"), None),
            P(("groups", "expert"), None),
            P(),
            P(),
            P("expert", None, None, "tensor"),
            P("expert", "tensor", None),
        ),
        out_specs=(
            P(("groups", "expert", "tensor"), None),
            P(("groups", "expert", "tensor"), None),
            P(("groups", "expert"), None, None, "tensor"),
            P(("groups", "expert"), "tensor", None),
        ),
        check_vma=False,
    )
```
